512 devices in a mesh: rows: 128 (over z, y, core), cols: 4 (over x).
Axes of the slice: x: 4, y: 8, z: 8, core: 2. Of those that a mesh axis runs over, the one named last changes fastest.
Arguments:
- right_sample: bfloat16 [32768, 320], P('rows', 'cols'), may hold values from -6 to 6
- left_sample: bfloat16 [32768, 320], P('rows', 'cols'), may hold values from -6 to 6
- updates: bfloat16 [128, 512, 512], P('rows'), may hold values from -0.25 to 0.25
- pattern: int32 [128, 4, 4], P('rows'), may hold values 0 or 1
- targets: int32 [128, 512], P('rows'), may hold values from 0 to 32767, as said below
- cluster_pos: int32 [32768], P('rows'), may hold values from 0 to 32767, as said below
- pivots: int32 [128, 128], P('rows'), may hold values from 0 to 255, as said below
Outputs:
- forward_out: float32 [32768, 320], P('rows', 'cols')
- transposed_out: float32 [32768, 320], P('rows', 'cols')
- interp: float32 [32768, 128], P('rows')
The draws below stay inside these ranges and needn't reach their ends.
Inputs may be any that keep to these rules, and one draw needn't show every extreme that they name: `targets`: the tile rows of one index of rows name at most 6 front rows held by any one index of rows; in every draw one index of rows receives exactly 6 from every index of rows. `cluster_pos`: A permutation; the 256 front rows of one index of rows take exactly 2 positions in the block of every index of rows. The pivots of one leaf are distinct.
All inputs are finite; a program needn't handle non-finite values. No bound on the sum of `pattern` on one device may be relied on, other than what follows from the above.
Results may differ from the reference program's by a relative error of at most 0.0003.
Values may be sent and summed in bfloat16 or wider, within the bound.
No kernel may reach another device: no remote copies, remote signals or barrier semaphores. Data moves between devices by JAX's collectives and lax.ppermute only.
A program may use at most 64 MiB of HBM per device.

```python
import jax
import jax.numpy as jnp
from jax import lax

ROWS_DEV = 256
K = 320
BLOCK = 512
TILE = 128
CHILD_DEV = 1
LEAF = 256
RANK = 128
M = 32768
CHILDREN = 128
CAP = 6
LEAVES = 128
N_ROWS = 128


def draw_targets(key, part):
    row_total = CHILD_DEV * BLOCK
    busy_owner = jax.random.randint(jax.random.fold_in(key, 7), (), 0, N_ROWS)

    def single(device_key):
        key_slots, key_order, key_offsets = jax.random.split(device_key, 3)
        chosen = jax.random.permutation(key_slots, (N_ROWS - 1) * CAP)[:row_total - CAP]
        owners = chosen // CAP
        owners = owners + (owners >= busy_owner).astype(jnp.int32)
        owners = jnp.concatenate([jnp.full((CAP,), busy_owner, jnp.int32), owners.astype(jnp.int32)])
        owners = jax.random.permutation(key_order, owners)
        offsets = jax.random.randint(key_offsets, (row_total,), 0, ROWS_DEV)
        return owners * ROWS_DEV + offsets
    device_keys = jax.random.split(jax.random.fold_in(key, 11), N_ROWS)
    return jax.vmap(single)(device_keys).reshape(CHILDREN, BLOCK).astype(jnp.int32)


def draw_cluster_pos(key, part):
    group_size = ROWS_DEV // N_ROWS
    sigma_keys = jax.random.split(jax.random.fold_in(key, 21), N_ROWS)
    tau_keys = jax.random.split(jax.random.fold_in(key, 22), N_ROWS)
    sigma = jax.vmap(lambda each_key: jax.random.permutation(each_key, ROWS_DEV))(sigma_keys)
    tau = jax.vmap(lambda each_key: jax.random.permutation(each_key, ROWS_DEV))(tau_keys)
    target_dev = sigma // group_size
    within = sigma % group_size
    arrival = jnp.arange(N_ROWS, dtype=jnp.int32)[:, None] * group_size + within
    landing = tau[target_dev, arrival]
    return (target_dev * ROWS_DEV + landing).reshape(M).astype(jnp.int32)


def draw_pivots(key, part):
    leaf_keys = jax.random.split(jax.random.fold_in(key, 31), LEAVES)
    chosen = jax.vmap(lambda each_key: jax.random.permutation(each_key, LEAF)[:RANK])(leaf_keys)
    return chosen.astype(jnp.int32)


def set_ends(entries, key, low, largest):
    extent = entries.shape
    place = [jax.random.randint(jax.random.fold_in(key, axis), (), 0, extent[axis]) for axis in range(len(extent))]
    entries = entries.at[tuple(place)].set(low)
    longest = extent.index(max(extent))
    place[longest] = (place[longest] + 1) % extent[longest]
    return entries.at[tuple(place)].set(largest)


def steps_of(rng, shape, cuts, least, largest):
    def one(position, blocks):
        heights = jax.random.uniform(jax.random.fold_in(jax.random.fold_in(rng, 6), position), (blocks,), jnp.float32, least / len(cuts), largest / len(cuts))
        return jnp.repeat(jnp.exp(heights), shape[position] // blocks).reshape((-1,) + (1,) * (len(shape) - position - 1))

    loudness = one(*cuts[0])
    for cut in cuts[1:]:
        loudness = loudness * one(*cut)
    return loudness


def scatter_about(rng, dims, deviation, reach, cuts=(), kind=jnp.bfloat16):
    result = deviation * jax.random.normal(rng, dims, jnp.float32)
    if cuts:
        result = result * steps_of(rng, dims, cuts, -0.22, 0.18)
    return jnp.clip(result, -reach, reach).astype(kind)


def setup_inputs(seed: int = 0) -> dict:
    key_list = jax.random.split(jax.random.key(seed), 8)
    right_sample = scatter_about(key_list[0], (M, K), 1.0, 6.0, ((0, 128), (1, 4)))
    left_sample = scatter_about(key_list[1], (M, K), 1.0, 6.0, ((0, 128), (1, 4)))
    updates = scatter_about(key_list[2], (CHILDREN, BLOCK, BLOCK), BLOCK ** -0.5, 0.25, ((0, 128),))
    pattern = set_ends((jax.random.randint(key_list[3], (CHILDREN, BLOCK // TILE, BLOCK // TILE), 0, 4) < 3).astype(jnp.int32), jax.random.fold_in(key_list[3], 1), 0, 1)
    targets = draw_targets(jax.random.fold_in(key_list[7], 71), 0)
    cluster_pos = draw_cluster_pos(jax.random.fold_in(key_list[7], 71), 0)
    pivots = draw_pivots(jax.random.fold_in(key_list[7], 71), 0)
    return dict(right_sample=right_sample, left_sample=left_sample, updates=updates, pattern=pattern, targets=targets, cluster_pos=cluster_pos, pivots=pivots)


def reference(right_sample, left_sample, updates, pattern, targets, cluster_pos, pivots):
    both_samples = jnp.concatenate([right_sample, left_sample], axis=1)

    def add_child(front_rows, inputs):
        update, tile_mask, child_rows = inputs
        full_mask = jnp.repeat(jnp.repeat(tile_mask, TILE, axis=0), TILE, axis=1)
        masked = jnp.where(full_mask != 0, update, jnp.zeros_like(update))
        picked = both_samples[child_rows]
        forward_part = jnp.dot(masked.astype(jnp.float32), picked[:, :K].astype(jnp.float32), preferred_element_type=jnp.float32)
        transposed_part = jnp.dot(masked.T.astype(jnp.float32), picked[:, K:].astype(jnp.float32), preferred_element_type=jnp.float32)
        contrib = jnp.concatenate([forward_part, transposed_part], axis=1)
        return (front_rows.at[child_rows].add(contrib), None)
    front_rows, unused = lax.scan(add_child, jnp.zeros((M, 2 * K), jnp.float32), (updates, pattern, targets))
    clustered = jnp.zeros((M, 2 * K), jnp.float32).at[cluster_pos].set(front_rows)
    by_leaf = clustered.reshape(LEAVES, LEAF, 2 * K)
    skeleton = jnp.take_along_axis(by_leaf, pivots[:, :, None], axis=1)
    gram_sum = jnp.einsum('lrk,lsk->lrs', skeleton, skeleton, precision=lax.Precision.HIGHEST)
    cross_sum = jnp.einsum('lik,lsk->lis', by_leaf, skeleton, precision=lax.Precision.HIGHEST)
    gram = gram_sum / (2.0 * K) + jnp.eye(RANK, dtype=jnp.float32)[None]
    factor = jnp.linalg.cholesky(gram)
    solved = jax.scipy.linalg.cho_solve((factor, True), jnp.swapaxes(cross_sum / (2.0 * K), 1, 2))
    interp = jnp.swapaxes(solved, 1, 2).reshape(M, RANK)
    return (clustered[:, :K], clustered[:, K:], interp)
```

```python
import jax
import jax.numpy as jnp
from jax import lax
from jax.experimental import pallas as pl
from jax.experimental.pallas import tpu as pltpu
from jax.sharding import PartitionSpec as P

K = 320
CAP = 6
F32 = jnp.float32
BF16 = jnp.bfloat16
NT = (((1,), (1,)), ((), ()))
NN = (((1,), (0,)), ((), ()))


def mm(a, b, dims=NN):
    return lax.dot_general(a, b, dims, preferred_element_type=F32)


def iota(shape, dim):
    return lax.broadcasted_iota(jnp.int32, shape, dim)


def split3(x):
    hi = x.astype(BF16)
    rest = x - hi.astype(F32)
    mid = rest.astype(BF16)
    low = (rest - mid.astype(F32)).astype(BF16)
    return hi, mid, low


def hot(mask):
    return jnp.where(mask, 1.0, 0.0).astype(BF16)


def ranks(keys, devices):
    n = keys.shape[1]
    member = keys == iota((devices, n), 0)
    ahead = hot(iota((n, n), 0) < iota((n, n), 1))
    return member, mm(hot(member), ahead)


def pick(member, rank, slot, values):
    chosen = jnp.where(jnp.logical_and(member, rank == float(slot)), values, 0.0)
    return jnp.sum(chosen, axis=1, keepdims=True)


def request_kernel(targets_ref, pos_ref, msg_ref, rows_ref):
    devices = msg_ref.shape[0]
    lanes = iota((devices, 128), 1)
    wanted = targets_ref[...]
    member, rank = ranks(wanted >> 8, devices)
    local = ((wanted & 255) + 1).astype(F32)
    msg = jnp.zeros((devices, 128), F32)
    for slot in range(CAP):
        msg = jnp.where(lanes == slot, pick(member, rank, slot, local) - 1.0, msg)
    pos = pos_ref[...]
    member, rank = ranks(pos >> 8, devices)
    landing = (pos & 255).astype(F32)
    here = iota(pos.shape, 1).astype(F32)
    rows = jnp.zeros((devices, 128), F32)
    for slot in range(2):
        msg = jnp.where(lanes == CAP + slot, pick(member, rank, slot, landing), msg)
        rows = jnp.where(lanes == slot, pick(member, rank, slot, here), rows)
    msg_ref[...] = msg.astype(jnp.int32)
    rows_ref[...] = rows.astype(jnp.int32)


def tile_prep_kernel(targets_ref, pattern_ref, updates_ref, slots_ref, masked_ref):
    devices = slots_ref.shape[0] // CAP
    member, rank = ranks(targets_ref[...] >> 8, devices)
    for slot in range(CAP):
        slots_ref[slot * devices : (slot + 1) * devices, :] = hot(
            jnp.logical_and(member, rank == float(slot))
        )
    for a in range(4):
        for b in range(4):
            part = updates_ref[a * 128 : (a + 1) * 128, b * 128 : (b + 1) * 128]
            keep = pattern_ref[a, b] != 0
            masked_ref[a * 128 : (a + 1) * 128, b * 128 : (b + 1) * 128] = jnp.where(
                keep, part, jnp.zeros_like(part)
            )


def front_prep_kernel(recv_ref, rows_ref, move_ref, land_ref):
    devices = recv_ref.shape[0]
    recv = recv_ref[...]
    across = jnp.transpose(recv.astype(F32)).astype(jnp.int32)
    for g in range(2):
        mine = rows_ref[:, g : g + 1]
        for slot in range(CAP):
            move_ref[
                g * devices : (g + 1) * devices, slot * devices : (slot + 1) * devices
            ] = hot(mine == across[slot : slot + 1, :])
        land_ref[g * devices : (g + 1) * devices, :] = hot(
            recv[:, CAP + g : CAP + g + 1] == iota((devices, land_ref.shape[1]), 1)
        )


def put_planes(ref, slot_rows, devices):
    part = [slot_rows[s * devices : (s + 1) * devices] for s in range(CAP)]
    for s in range(CAP):
        ref[pl.ds(s, devices, stride=8), :] = part[s][:, :128]
    ref[pl.ds(6, devices, stride=8), :] = jnp.concatenate(
        [part[s][:, 128:160] for s in range(4)], axis=1
    )
    ref[pl.ds(7, devices, stride=8), :] = jnp.concatenate(
        [part[4][:, 128:160], part[5][:, 128:160], jnp.zeros((devices, 64), F32)], axis=1
    )


def reply_kernel(recv_ref, right_ref, left_ref, out_ref, scratch):
    devices = recv_ref.shape[0]
    samples = jnp.concatenate([right_ref[...], left_ref[...]], axis=0)
    places = iota((devices, samples.shape[1]), 1)
    chosen = jnp.concatenate(
        [hot(recv_ref[:, s : s + 1] == places) for s in range(CAP)], axis=0
    )
    put_planes(scratch, mm(chosen, samples, NT), devices)
    out_ref[...] = scratch[...].reshape(out_ref.shape).astype(BF16)


def tile_kernel(fetched_ref, slots_ref, masked_ref, out_ref, scratch):
    devices = fetched_ref.shape[0]
    scratch[...] = fetched_ref[...].astype(F32).reshape(scratch.shape)
    across = [
        jnp.transpose(scratch[pl.ds(s, devices, stride=8), :]) for s in range(8)
    ]
    columns = jnp.concatenate(
        [
            jnp.concatenate(
                [across[s], across[6 + s // 4][32 * (s % 4) : 32 * (s % 4) + 32]], axis=0
            )
            for s in range(CAP)
        ],
        axis=1,
    ).astype(BF16)
    slots = slots_ref[...]
    gathered = mm(columns, slots).astype(BF16)
    masked = masked_ref[...]
    half = gathered.shape[0] // 2
    forward = mm(gathered[:half], masked, NT)
    transposed = mm(gathered[half:], masked, NN)
    contrib = split3(jnp.concatenate([forward, transposed], axis=0))
    sent = mm(slots, contrib[0], NT) + mm(slots, contrib[1], NT) + mm(slots, contrib[2], NT)
    put_planes(out_ref, sent, devices)


def front_kernel(incoming_ref, move_ref, out_ref):
    devices = out_ref.shape[0]
    plane = [incoming_ref[pl.ds(s, devices, stride=8), :] for s in range(8)]
    main = split3(jnp.concatenate(plane[:CAP], axis=0))
    rest = split3(
        jnp.concatenate(
            [plane[6 + s // 4][:, 32 * (s % 4) : 32 * (s % 4) + 32] for s in range(CAP)],
            axis=0,
        )
    )
    move = move_ref[...]
    main = mm(move, main[0]) + mm(move, main[1]) + mm(move, main[2])
    rest = mm(move, rest[0]) + mm(move, rest[1]) + mm(move, rest[2])
    out_ref[:, 0:128] = main[:devices]
    out_ref[:, 128:256] = main[devices:]
    out_ref[:, 256:384] = jnp.concatenate(
        [rest[:devices], rest[devices:], jnp.zeros((devices, 64), F32)], axis=1
    )


def cluster_kernel(arrived_ref, land_ref, forward_ref, transposed_ref, joined_ref):
    first = jnp.transpose(arrived_ref[:, 0:128])
    second = jnp.transpose(arrived_ref[:, 128:256])
    rest = jnp.transpose(arrived_ref[:, 256:384])
    columns = jnp.concatenate(
        [
            jnp.concatenate([first, rest[0:32]], axis=0),
            jnp.concatenate([second, rest[32:64]], axis=0),
        ],
        axis=1,
    )
    land = land_ref[...]
    parts = split3(columns)
    joined = mm(parts[0], land) + mm(parts[1], land) + mm(parts[2], land)
    half = joined.shape[0] // 2
    forward_ref[...] = joined[:half]
    transposed_ref[...] = joined[half:]
    joined_ref[...] = joined


def mm_full(a, b):
    a0, a1, a2 = split3(a)
    b0, b1, b2 = split3(b)
    return (
        (mm(a2, b0) + mm(a1, b1) + mm(a0, b2)) + (mm(a1, b0) + mm(a0, b1))
    ) + mm(a0, b0)


def mm_hot(a, b):
    a0, a1, a2 = split3(a)
    return mm(a0, b) + mm(a1, b) + mm(a2, b)


def inverse(a):
    n = a.shape[0]
    sub, lane = iota(a.shape, 0), iota(a.shape, 1)
    for k in range(n):
        pivot = 1.0 / a[k : k + 1, k : k + 1]
        row = jnp.where(lane[k : k + 1] == k, 1.0, a[k : k + 1, :]) * pivot
        column = jnp.where(sub[:, 0:1] == k, -1.0, a[:, k : k + 1])
        rest = jnp.where(jnp.logical_or(sub == k, lane == k), 0.0, a)
        a = rest - column * row
    return a


def leaf_kernel(joined_ref, pivots_ref, interp_ref):
    joined = joined_ref[...]
    leaf, rank = joined.shape[1], pivots_ref.shape[1]
    chosen = hot(iota((leaf, rank), 0) == pivots_ref[...])
    skeleton = jnp.transpose(mm_hot(joined, chosen))
    cross = mm_full(skeleton, joined) * (1.0 / (2.0 * K))
    eye = jnp.where(iota((rank, rank), 0) == iota((rank, rank), 1), 1.0, 0.0)
    gram = mm_hot(cross, chosen) + eye
    interp_ref[...] = mm_full(jnp.transpose(cross), inverse(gram))


def call(kernel, outs, *args, scratch=(), smem=(), flops=1_000_000):
    spec = [
        pl.BlockSpec(memory_space=pltpu.SMEM if i in smem else pltpu.VMEM)
        for i in range(len(args))
    ]
    return pl.pallas_call(
        kernel,
        out_shape=outs,
        in_specs=spec,
        out_specs=jax.tree.map(lambda _: pl.BlockSpec(memory_space=pltpu.VMEM), outs),
        scratch_shapes=scratch,
        compiler_params=pltpu.CompilerParams(vmem_limit_bytes=48 * 2**20),
        cost_estimate=pl.CostEstimate(
            flops=flops, bytes_accessed=1_000_000, transcendentals=0
        ),
    )(*args)


def per_device(right_sample, left_sample, updates, pattern, targets, cluster_pos, pivots):
    devices = lax.axis_size("rows")
    local_rows, width = right_sample.shape
    block = updates.shape[1]
    shape = jax.ShapeDtypeStruct

    def exchange(x):
        return lax.all_to_all(x, "rows", split_axis=0, concat_axis=0, tiled=True)

    message, front_order = call(
        request_kernel,
        [shape((devices, 128), jnp.int32), shape((devices, 128), jnp.int32)],
        targets,
        cluster_pos.reshape(1, local_rows),
    )
    received = exchange(message)
    slots, masked = call(
        tile_prep_kernel,
        [shape((CAP * devices, block), BF16), shape((block, block), BF16)],
        targets,
        pattern[0],
        updates[0],
        smem=(1,),
    )
    reply = call(
        reply_kernel,
        shape((devices, 8, 128), BF16),
        received,
        right_sample.T,
        left_sample.T,
        scratch=[pltpu.VMEM((devices * 8, 128), F32)],
    )
    fetched = exchange(reply)
    move, land = call(
        front_prep_kernel,
        [
            shape((2 * devices, CAP * devices), BF16),
            shape((2 * devices, local_rows), BF16),
        ],
        received,
        front_order,
    )
    outgoing = call(
        tile_kernel,
        shape((devices * 8, 128), F32),
        fetched,
        slots,
        masked,
        scratch=[pltpu.VMEM((devices * 8, 128), F32)],
    )
    incoming = exchange(outgoing.reshape(devices, 8, 128)).reshape(devices * 8, 128)
    moved = call(front_kernel, shape((devices, 384), F32), incoming, move)
    arrived = exchange(moved)
    forward, transposed, joined = call(
        cluster_kernel,
        [
            shape((width, local_rows), F32),
            shape((width, local_rows), F32),
            shape((2 * width, local_rows), F32),
        ],
        arrived,
        land,
    )
    columns = lax.axis_size("cols")
    spread = lax.all_to_all(
        jnp.broadcast_to(joined[None], (columns,) + joined.shape),
        "cols",
        split_axis=0,
        concat_axis=0,
        tiled=True,
    )
    interp = call(
        leaf_kernel,
        shape((local_rows, pivots.shape[1]), F32),
        spread.reshape(columns * 2 * width, local_rows),
        pivots,
    )
    return forward.T, transposed.T, interp


def solution(mesh):
    return jax.shard_map(
        per_device,
        mesh=mesh,
        in_specs=(
            P("rows", "cols"),
            P("rows", "cols"),
            P("rows", None, None),
            P("rows", None, None),
            P("rows", None),
            P("rows"),
            P("rows", None),
        ),
        out_specs=(P("rows", "cols"), P("rows", "cols"), P("rows", None)),
        check_vma=False,
    )
```

```python
import jax
import jax.numpy as jnp
from jax import lax
from jax.experimental import pallas as pl
from jax.experimental.pallas import tpu as pltpu
from jax.sharding import PartitionSpec as P

K = 320
CAP = 6
HALF = 80
CODES = 64
LOG2 = 0.6931471805599453
F32 = jnp.float32
BF16 = jnp.bfloat16
NT = (((1,), (1,)), ((), ()))
NN = (((1,), (0,)), ((), ()))


def mm(a, b, dims=NN):
    return lax.dot_general(a, b, dims, preferred_element_type=F32)


def iota(shape, dim):
    return lax.broadcasted_iota(jnp.int32, shape, dim)


def split3(x):
    hi = x.astype(BF16)
    rest = x - hi.astype(F32)
    mid = rest.astype(BF16)
    low = (rest - mid.astype(F32)).astype(BF16)
    return hi, mid, low


def hot(mask):
    return jnp.where(mask, 1.0, 0.0).astype(BF16)


def ranks(keys, devices):
    n = keys.shape[1]
    member = keys == iota((devices, n), 0)
    ahead = hot(iota((n, n), 0) < iota((n, n), 1))
    return member, mm(hot(member), ahead)


def pick(member, rank, slot, values):
    chosen = jnp.where(jnp.logical_and(member, rank == float(slot)), values, 0.0)
    return jnp.sum(chosen, axis=1, keepdims=True)


def request_kernel(
    targets_hbm, pos_hbm, msg_ref, rows_ref, targets_ref, pos_ref, arrivals
):
    devices = msg_ref.shape[0]
    first = pltpu.make_async_copy(targets_hbm, targets_ref, arrivals.at[0])
    second = pltpu.make_async_copy(pos_hbm, pos_ref, arrivals.at[1])
    first.start()
    second.start()
    first.wait()
    second.wait()
    lanes = iota((devices, 128), 1)
    wanted = targets_ref[...]
    member, rank = ranks(wanted >> 8, devices)
    local = ((wanted & 255) + 1).astype(F32)
    msg = jnp.zeros((devices, 128), F32)
    for slot in range(CAP):
        msg = jnp.where(lanes == slot, pick(member, rank, slot, local) - 1.0, msg)
    pos = pos_ref[...]
    member, rank = ranks(pos >> 8, devices)
    landing = (pos & 255).astype(F32)
    here = iota(pos.shape, 1).astype(F32)
    rows = jnp.zeros((devices, 128), F32)
    for slot in range(2):
        msg = jnp.where(lanes == CAP + slot, pick(member, rank, slot, landing), msg)
        rows = jnp.where(lanes == slot, pick(member, rank, slot, here), rows)
    msg_ref[...] = msg.astype(jnp.int32)
    rows_ref[...] = rows.astype(jnp.int32)


def tile_prep_kernel(
    targets_ref, pattern_ref, updates_ref, slots_ref, member_ref, rank_ref, masked_ref
):
    devices = member_ref.shape[0]
    member, rank = ranks(targets_ref[...] >> 8, devices)
    member_ref[...] = hot(member)
    rank_ref[...] = jnp.broadcast_to(
        jnp.sum(jnp.where(member, rank, 0.0), axis=0, keepdims=True), rank_ref.shape
    )
    for slot in range(CAP):
        slots_ref[slot * devices : (slot + 1) * devices, :] = hot(
            jnp.logical_and(member, rank == float(slot))
        )
    for a in range(4):
        for b in range(4):
            part = updates_ref[a * 128 : (a + 1) * 128, b * 128 : (b + 1) * 128]
            keep = pattern_ref[a, b] != 0
            masked_ref[a * 128 : (a + 1) * 128, b * 128 : (b + 1) * 128] = jnp.where(
                keep, part, jnp.zeros_like(part)
            )


def front_prep_kernel(
    recv_ref, rows_ref, pivots_ref, move_ref, land_ref, scale_ref, chosen_ref
):
    devices = recv_ref.shape[0]
    recv = recv_ref[...]
    across = jnp.transpose(recv.astype(F32)).astype(jnp.int32)
    for g in range(2):
        mine = rows_ref[:, g : g + 1]
        for slot in range(CAP):
            move_ref[
                g * devices : (g + 1) * devices, slot * devices : (slot + 1) * devices
            ] = hot(mine == across[slot : slot + 1, :])
        land_ref[g * devices : (g + 1) * devices, :] = hot(
            recv[:, CAP + g : CAP + g + 1] == iota((devices, land_ref.shape[1]), 1)
        )
    place, lane = iota((128, 128), 0), iota((128, 128), 1)
    for s in range(CAP):
        scale_ref[:, 128 * s : 128 * s + 128] = hot(
            place == CODES + s + jnp.where(lane >= HALF, 8, 0)
        )
    for s in (6, 7):
        scale_ref[:, 128 * s : 128 * s + 128] = hot(
            place == CODES + 8 + 4 * (s - 6) + (lane >> 5)
        )
    chosen_ref[...] = hot(iota(chosen_ref.shape, 0) == pivots_ref[...])


def reply_kernel(recv_ref, right_ref, left_ref, out_ref, scratch):
    devices = recv_ref.shape[0]
    samples = jnp.concatenate([right_ref[...], left_ref[...]], axis=0)
    places = iota((devices, samples.shape[1]), 1)
    chosen = jnp.concatenate(
        [hot(recv_ref[:, s : s + 1] == places) for s in range(CAP)], axis=0
    )
    rows = mm(chosen, samples, NT)
    part = [rows[s * devices : (s + 1) * devices] for s in range(CAP)]
    for s in range(CAP):
        scratch[pl.ds(s, devices, stride=8), :] = part[s][:, :128]
    scratch[pl.ds(6, devices, stride=8), :] = jnp.concatenate(
        [part[s][:, 128:160] for s in range(4)], axis=1
    )
    scratch[pl.ds(7, devices, stride=8), :] = jnp.concatenate(
        [part[4][:, 128:160], part[5][:, 128:160], jnp.zeros((devices, 64), F32)], axis=1
    )
    out_ref[...] = scratch[...].reshape(out_ref.shape).astype(BF16)


def steps_of(code):
    return jnp.exp(code * (LOG2 / 256.0)) * (1.0 / 32600.0)


def coded(x):
    peak = jnp.maximum(jnp.max(jnp.abs(x), axis=0, keepdims=True), 1e-32)
    code = jnp.ceil(jnp.log(peak) * (256.0 / LOG2))
    return jnp.floor(x / steps_of(code) + 0.5), code


def mm_whole(hots, x):
    high = jnp.floor(x * (1.0 / 256.0) + 0.5)
    low = x - 256.0 * high
    return mm(hots, high.astype(BF16), NT) * 256.0 + mm(hots, low.astype(BF16), NT)


def tile_kernel(
    fetched_ref, slots_ref, member_ref, rank_ref, masked_ref, out_ref, scratch
):
    devices, columns = member_ref.shape
    scratch[...] = fetched_ref[...].astype(F32).reshape(scratch.shape)
    across = [
        jnp.transpose(scratch[pl.ds(s, devices, stride=8), :]).astype(BF16)
        for s in range(8)
    ]
    slots, member, rank = slots_ref[...], member_ref[...], rank_ref[0:1, :]
    main = mm(jnp.concatenate(across[:CAP], axis=1), slots)
    rest = mm(jnp.concatenate(across[CAP:], axis=0), member)
    tail = jnp.zeros((32, columns), F32)
    for s in range(CAP):
        tail = jnp.where(rank == float(s), rest[32 * s : 32 * s + 32], tail)
    gathered = jnp.concatenate([main, tail], axis=0).astype(BF16)
    masked = masked_ref[...]
    forward, forward_code = coded(mm(gathered[:HALF], masked, NT))
    transposed, transposed_code = coded(mm(gathered[HALF:], masked, NN))
    tail = transposed[128 - HALF :]
    row = iota((8, columns), 0).astype(F32)
    rest = jnp.concatenate(
        [jnp.where(rank == float(s), tail, 0.0) for s in range(CAP)]
        + [
            jnp.where(rank == row, forward_code, 0.0),
            jnp.where(rank == row, transposed_code, 0.0),
            jnp.zeros((48, columns), F32),
        ],
        axis=0,
    )
    main = mm_whole(slots, jnp.concatenate([forward, transposed[: 128 - HALF]], axis=0))
    rest = mm_whole(member, rest)
    for s in range(CAP):
        scratch[pl.ds(s, devices, stride=8), :] = main[s * devices : (s + 1) * devices]
    scratch[pl.ds(6, devices, stride=8), :] = rest[:, :128]
    scratch[pl.ds(7, devices, stride=8), :] = rest[:, 128:]
    out_ref[...] = (
        scratch[...].reshape(out_ref.shape).astype(jnp.int32).astype(jnp.int16)
    )


def front_kernel(incoming_ref, move_ref, scale_ref, out_ref, scratch):
    devices = out_ref.shape[0]
    scratch[...] = (
        incoming_ref[...].astype(jnp.int32).astype(F32).reshape(scratch.shape)
    )
    plane = [scratch[pl.ds(s, devices, stride=8), :] for s in range(8)]
    codes = jnp.where(iota(plane[7].shape, 1) >= CODES, plane[7], 0.0)
    scales = mm_hot(steps_of(codes), scale_ref[...])
    plane = [plane[s] * scales[:, 128 * s : 128 * s + 128] for s in range(8)]
    main = split3(jnp.concatenate(plane[:CAP], axis=0))
    rest = split3(
        jnp.concatenate(
            [plane[6 + s // 4][:, 32 * (s % 4) : 32 * (s % 4) + 32] for s in range(CAP)],
            axis=0,
        )
    )
    move = move_ref[...]
    main = mm(move, main[0]) + mm(move, main[1]) + mm(move, main[2])
    rest = mm(move, rest[0]) + mm(move, rest[1]) + mm(move, rest[2])
    out_ref[:, 0:128] = main[:devices]
    out_ref[:, 128:256] = main[devices:]
    out_ref[:, 256:384] = jnp.concatenate(
        [rest[:devices], rest[devices:], jnp.zeros((devices, 64), F32)], axis=1
    )


def cluster_kernel(arrived_ref, land_ref, forward_ref, transposed_ref, joined_ref):
    first = jnp.transpose(arrived_ref[:, 0:128])
    second = jnp.transpose(arrived_ref[:, 128:256])
    rest = jnp.transpose(arrived_ref[:, 256:384])
    columns = jnp.concatenate(
        [
            jnp.concatenate([first, rest[0:32]], axis=0),
            jnp.concatenate([second, rest[32:64]], axis=0),
        ],
        axis=1,
    )
    land = land_ref[...]
    parts = split3(columns)
    joined = mm(parts[0], land) + mm(parts[1], land) + mm(parts[2], land)
    half = joined.shape[0] // 2
    forward_ref[...] = joined[:half]
    transposed_ref[...] = joined[half:]
    joined_ref[...] = joined


def mm_full(a, b):
    a0, a1, a2 = split3(a)
    b0, b1, b2 = split3(b)
    return (
        (mm(a2, b0) + mm(a1, b1) + mm(a0, b2)) + (mm(a1, b0) + mm(a0, b1))
    ) + mm(a0, b0)


def mm_hot(a, b):
    a0, a1, a2 = split3(a)
    return mm(a0, b) + mm(a1, b) + mm(a2, b)


def small_inverse(p, n):
    def at(d, i, j):
        return d[min(i, j), max(i, j)]

    if n == 1:
        return {(0, 0): 1.0 / p[0, 0]}
    if n == 2:
        a, b, c = p[0, 0], p[0, 1], p[1, 1]
        r = 1.0 / (a * c - b * b)
        return {(0, 0): c * r, (0, 1): -b * r, (1, 1): a * r}
    h = n // 2
    pairs = [(i, j) for i in range(h) for j in range(i, h)]
    first = small_inverse({(i, j): p[i, j] for i, j in pairs}, h)
    w = {
        (i, j): sum(at(first, i, k) * p[k, h + j] for k in range(h))
        for i in range(h)
        for j in range(h)
    }
    second = small_inverse(
        {
            (i, j): p[h + i, h + j] - sum(p[k, h + i] * w[k, j] for k in range(h))
            for i, j in pairs
        },
        h,
    )
    t = {
        (i, j): sum(w[i, k] * at(second, k, j) for k in range(h))
        for i in range(h)
        for j in range(h)
    }
    out = {(i, h + j): -t[i, j] for i in range(h) for j in range(h)}
    for i, j in pairs:
        out[i, j] = first[i, j] + sum(t[i, k] * w[j, k] for k in range(h))
        out[h + i, h + j] = second[i, j]
    return out


def inverse(matrix, b=4):
    n = matrix.shape[0]
    a = [matrix[8 * i : 8 * i + 8] for i in range(n // 8)]
    shape = a[0].shape
    sub, lane = iota(shape, 0), iota(shape, 1)

    def spread(x):
        return jnp.broadcast_to(x, shape)

    for k in range(0, n, b):
        group, o = divmod(k, 8)
        rows = [spread(a[group][o + q : o + q + 1, :]) for q in range(b)]
        pivot = small_inverse(
            {
                (q, r): spread(rows[q][:, k + r : k + r + 1])
                for q in range(b)
                for r in range(q, b)
            },
            b,
        )
        inside = jnp.logical_and(lane >= k, lane < k + b)
        rows = [
            jnp.where(inside, jnp.where(lane == k + q, 1.0, 0.0), rows[q])
            for q in range(b)
        ]
        new = [
            sum(pivot[min(q, r), max(q, r)] * rows[r] for r in range(b))
            for q in range(b)
        ]
        mine = jnp.logical_and(sub >= o, sub < o + b)
        for i in range(n // 8):
            total = jnp.where(inside, 0.0, a[i])
            for q in range(b):
                total = total - spread(a[i][:, k + q : k + q + 1]) * new[q]
            if i == group:
                picked = new[0]
                for q in range(1, b):
                    picked = jnp.where(sub == o + q, new[q], picked)
                total = jnp.where(mine, picked, total)
            a[i] = total
    return jnp.concatenate(a, axis=0)


def leaf_kernel(joined_ref, chosen_ref, interp_ref):
    joined, chosen = joined_ref[...], chosen_ref[...]
    rank = chosen.shape[1]
    skeleton = jnp.transpose(mm_hot(joined, chosen))
    cross = mm_full(skeleton, joined) * (1.0 / (2.0 * K))
    eye = jnp.where(iota((rank, rank), 0) == iota((rank, rank), 1), 1.0, 0.0)
    gram = mm_hot(cross, chosen) + eye
    interp_ref[...] = mm_full(jnp.transpose(cross), inverse(gram))


def call(kernel, outs, *args, scratch=(), smem=(), hbm=(), flops=1_000_000):
    spec = [
        pl.BlockSpec(
            memory_space=pltpu.SMEM if i in smem else pltpu.HBM if i in hbm else pltpu.VMEM
        )
        for i in range(len(args))
    ]
    return pl.pallas_call(
        kernel,
        out_shape=outs,
        in_specs=spec,
        out_specs=jax.tree.map(lambda _: pl.BlockSpec(memory_space=pltpu.VMEM), outs),
        scratch_shapes=scratch,
        compiler_params=pltpu.CompilerParams(vmem_limit_bytes=48 * 2**20),
        cost_estimate=pl.CostEstimate(
            flops=flops, bytes_accessed=1_000_000, transcendentals=0
        ),
    )(*args)


def per_device(right_sample, left_sample, updates, pattern, targets, cluster_pos, pivots):
    devices = lax.axis_size("rows")
    local_rows, width = right_sample.shape
    block = updates.shape[1]
    shape = jax.ShapeDtypeStruct

    def exchange(x):
        return lax.all_to_all(x, "rows", split_axis=0, concat_axis=0, tiled=True)

    message, front_order = call(
        request_kernel,
        [shape((devices, 128), jnp.int32), shape((devices, 128), jnp.int32)],
        targets,
        cluster_pos.reshape(1, local_rows),
        hbm=(0, 1),
        scratch=[
            pltpu.VMEM((1, block), jnp.int32),
            pltpu.VMEM((1, local_rows), jnp.int32),
            pltpu.SemaphoreType.DMA((2,)),
        ],
    )
    received = exchange(message)
    slots, member, rank, masked = call(
        tile_prep_kernel,
        [
            shape((CAP * devices, block), BF16),
            shape((devices, block), BF16),
            shape((8, block), F32),
            shape((block, block), BF16),
        ],
        targets,
        pattern[0],
        updates[0],
        smem=(1,),
    )
    reply = call(
        reply_kernel,
        shape((devices, 8, 128), BF16),
        received,
        right_sample.T,
        left_sample.T,
        scratch=[pltpu.VMEM((devices * 8, 128), F32)],
    )
    fetched = exchange(reply)
    move, land, scale, chosen = call(
        front_prep_kernel,
        [
            shape((2 * devices, CAP * devices), BF16),
            shape((2 * devices, local_rows), BF16),
            shape((128, 1024), BF16),
            shape((local_rows, pivots.shape[1]), BF16),
        ],
        received,
        front_order,
        pivots,
    )
    outgoing = call(
        tile_kernel,
        shape((devices, 8, 128), jnp.int16),
        fetched,
        slots,
        member,
        rank,
        masked,
        scratch=[pltpu.VMEM((devices * 8, 128), F32)],
    )
    incoming = exchange(outgoing)
    moved = call(
        front_kernel,
        shape((devices, 384), F32),
        incoming,
        move,
        scale,
        scratch=[pltpu.VMEM((devices * 8, 128), F32)],
    )
    arrived = exchange(moved)
    forward, transposed, joined = call(
        cluster_kernel,
        [
            shape((width, local_rows), F32),
            shape((width, local_rows), F32),
            shape((2 * width, local_rows), F32),
        ],
        arrived,
        land,
    )
    columns = lax.axis_size("cols")
    spread = lax.all_to_all(
        jnp.broadcast_to(joined[None], (columns,) + joined.shape),
        "cols",
        split_axis=0,
        concat_axis=0,
        tiled=True,
    )
    interp = call(
        leaf_kernel,
        shape((local_rows, pivots.shape[1]), F32),
        spread.reshape(columns * 2 * width, local_rows),
        chosen,
    )
    return forward.T, transposed.T, interp


def solution(mesh):
    return jax.shard_map(
        per_device,
        mesh=mesh,
        in_specs=(
            P("rows", "cols"),
            P("rows", "cols"),
            P("rows", None, None),
            P("rows", None, None),
            P("rows", None),
            P("rows"),
            P("rows", None),
        ),
        out_specs=(P("rows", "cols"), P("rows", "cols"), P("rows", None)),
        check_vma=False,
    )
```

```python
import jax
import jax.numpy as jnp
from jax import lax
from jax.experimental import pallas as pl
from jax.experimental.pallas import tpu as pltpu
from jax.sharding import PartitionSpec as P

K = 320
CAP = 6
HALF = 80
CODES = 64
LOG2 = 0.6931471805599453
F32 = jnp.float32
BF16 = jnp.bfloat16
NT = (((1,), (1,)), ((), ()))
NN = (((1,), (0,)), ((), ()))


def mm(a, b, dims=NN):
    return lax.dot_general(a, b, dims, preferred_element_type=F32)


def iota(shape, dim):
    return lax.broadcasted_iota(jnp.int32, shape, dim)


def split3(x):
    hi = x.astype(BF16)
    rest = x - hi.astype(F32)
    mid = rest.astype(BF16)
    low = (rest - mid.astype(F32)).astype(BF16)
    return hi, mid, low


def hot(mask):
    return jnp.where(mask, 1.0, 0.0).astype(BF16)


def ranks(keys, devices):
    n = keys.shape[1]
    member = keys == iota((devices, n), 0)
    ahead = hot(iota((n, n), 0) < iota((n, n), 1))
    return member, mm(hot(member), ahead)


def pick(member, rank, slot, values):
    chosen = jnp.where(jnp.logical_and(member, rank == float(slot)), values, 0.0)
    return jnp.sum(chosen, axis=1, keepdims=True)


def request_kernel(
    targets_hbm, pos_hbm, msg_ref, rows_ref, targets_ref, pos_ref, arrivals
):
    devices = msg_ref.shape[0]
    first = pltpu.make_async_copy(targets_hbm, targets_ref, arrivals.at[0])
    second = pltpu.make_async_copy(pos_hbm, pos_ref, arrivals.at[1])
    first.start()
    second.start()
    first.wait()
    second.wait()
    lanes = iota((devices, 128), 1)
    wanted = targets_ref[...]
    member, rank = ranks(wanted >> 8, devices)
    local = ((wanted & 255) + 1).astype(F32)
    msg = jnp.zeros((devices, 128), F32)
    for slot in range(CAP):
        msg = jnp.where(lanes == slot, pick(member, rank, slot, local) - 1.0, msg)
    pos = pos_ref[...]
    member, rank = ranks(pos >> 8, devices)
    landing = (pos & 255).astype(F32)
    here = iota(pos.shape, 1).astype(F32)
    rows = jnp.zeros((devices, 128), F32)
    for slot in range(2):
        msg = jnp.where(lanes == CAP + slot, pick(member, rank, slot, landing), msg)
        rows = jnp.where(lanes == slot, pick(member, rank, slot, here), rows)
    msg_ref[...] = msg.astype(jnp.int32)
    rows_ref[...] = rows.astype(jnp.int32)


def tile_prep_kernel(
    targets_ref, pattern_ref, updates_ref, slots_ref, member_ref, rank_ref, masked_ref
):
    devices = member_ref.shape[0]
    member, rank = ranks(targets_ref[...] >> 8, devices)
    member_ref[...] = hot(member)
    rank_ref[...] = jnp.broadcast_to(
        jnp.sum(jnp.where(member, rank, 0.0), axis=0, keepdims=True), rank_ref.shape
    )
    for slot in range(CAP):
        slots_ref[slot * devices : (slot + 1) * devices, :] = hot(
            jnp.logical_and(member, rank == float(slot))
        )
    for a in range(4):
        for b in range(4):
            part = updates_ref[a * 128 : (a + 1) * 128, b * 128 : (b + 1) * 128]
            keep = pattern_ref[a, b] != 0
            masked_ref[a * 128 : (a + 1) * 128, b * 128 : (b + 1) * 128] = jnp.where(
                keep, part, jnp.zeros_like(part)
            )


def front_prep_kernel(
    recv_ref, rows_ref, pivots_ref, move_ref, land_ref, leaf_land_ref, scale_ref, order_ref
):
    devices = recv_ref.shape[0]
    leaf, rank = land_ref.shape[1], pivots_ref.shape[1]
    recv = recv_ref[...]
    across = jnp.transpose(recv.astype(F32)).astype(jnp.int32)
    for g in range(2):
        mine = rows_ref[:, g : g + 1]
        for slot in range(CAP):
            move_ref[
                g * devices : (g + 1) * devices, slot * devices : (slot + 1) * devices
            ] = hot(mine == across[slot : slot + 1, :])
        land_ref[g * devices : (g + 1) * devices, :] = hot(
            recv[:, CAP + g : CAP + g + 1] == iota((devices, leaf), 1)
        )
    pivot = iota((leaf, rank), 0) == pivots_ref[...]
    other = 1.0 - jnp.sum(jnp.where(pivot, 1.0, 0.0), axis=1, keepdims=True)
    other = jnp.broadcast_to(other, (leaf, leaf - rank))
    ahead = mm(hot(iota((leaf, leaf), 1) < iota((leaf, leaf), 0)), other.astype(BF16))
    order_ref[:, :rank] = hot(pivot)
    order_ref[:, rank:] = hot(
        jnp.logical_and(other > 0.5, ahead == iota(ahead.shape, 1).astype(F32))
    )
    leaf_land_ref[...] = jnp.transpose(mm(land_ref[...], order_ref[...])).astype(BF16)
    place, lane = iota((128, 128), 0), iota((128, 128), 1)
    for s in range(CAP):
        scale_ref[:, 128 * s : 128 * s + 128] = hot(
            place == CODES + s + jnp.where(lane >= HALF, 8, 0)
        )
    for s in (6, 7):
        scale_ref[:, 128 * s : 128 * s + 128] = hot(
            place == CODES + 8 + 4 * (s - 6) + (lane >> 5)
        )

def reply_kernel(recv_ref, right_ref, left_ref, out_ref, scratch):
    devices = recv_ref.shape[0]
    samples = jnp.concatenate([right_ref[...], left_ref[...]], axis=0)
    places = iota((devices, samples.shape[1]), 1)
    chosen = jnp.concatenate(
        [hot(recv_ref[:, s : s + 1] == places) for s in range(CAP)], axis=0
    )
    rows = mm(chosen, samples, NT)
    part = [rows[s * devices : (s + 1) * devices] for s in range(CAP)]
    for s in range(CAP):
        scratch[pl.ds(s, devices, stride=8), :] = part[s][:, :128]
    scratch[pl.ds(6, devices, stride=8), :] = jnp.concatenate(
        [part[s][:, 128:160] for s in range(4)], axis=1
    )
    scratch[pl.ds(7, devices, stride=8), :] = jnp.concatenate(
        [part[4][:, 128:160], part[5][:, 128:160], jnp.zeros((devices, 64), F32)], axis=1
    )
    out_ref[...] = scratch[...].reshape(out_ref.shape).astype(BF16)


def steps_of(code):
    return jnp.exp(code * (LOG2 / 256.0)) * (1.0 / 32600.0)


def coded(x):
    peak = jnp.maximum(jnp.max(jnp.abs(x), axis=0, keepdims=True), 1e-32)
    code = jnp.ceil(jnp.log(peak) * (256.0 / LOG2))
    return jnp.floor(x / steps_of(code) + 0.5), code


def mm_whole(hots, x):
    high = jnp.floor(x * (1.0 / 256.0) + 0.5)
    low = x - 256.0 * high
    return mm(hots, high.astype(BF16), NT) * 256.0 + mm(hots, low.astype(BF16), NT)


def tile_kernel(
    fetched_ref, slots_ref, member_ref, rank_ref, masked_ref, out_ref, scratch
):
    devices, columns = member_ref.shape
    scratch[...] = fetched_ref[...].astype(F32).reshape(scratch.shape)
    across = [
        jnp.transpose(scratch[pl.ds(s, devices, stride=8), :]).astype(BF16)
        for s in range(8)
    ]
    slots, member, rank = slots_ref[...], member_ref[...], rank_ref[0:1, :]
    main = mm(jnp.concatenate(across[:CAP], axis=1), slots)
    rest = mm(jnp.concatenate(across[CAP:], axis=0), member)
    tail = jnp.zeros((32, columns), F32)
    for s in range(CAP):
        tail = jnp.where(rank == float(s), rest[32 * s : 32 * s + 32], tail)
    gathered = jnp.concatenate([main, tail], axis=0).astype(BF16)
    masked = masked_ref[...]
    forward, forward_code = coded(mm(gathered[:HALF], masked, NT))
    transposed, transposed_code = coded(mm(gathered[HALF:], masked, NN))
    tail = transposed[128 - HALF :]
    row = iota((8, columns), 0).astype(F32)
    rest = jnp.concatenate(
        [jnp.where(rank == float(s), tail, 0.0) for s in range(CAP)]
        + [
            jnp.where(rank == row, forward_code, 0.0),
            jnp.where(rank == row, transposed_code, 0.0),
            jnp.zeros((48, columns), F32),
        ],
        axis=0,
    )
    main = mm_whole(slots, jnp.concatenate([forward, transposed[: 128 - HALF]], axis=0))
    rest = mm_whole(member, rest)
    for s in range(CAP):
        scratch[pl.ds(s, devices, stride=8), :] = main[s * devices : (s + 1) * devices]
    scratch[pl.ds(6, devices, stride=8), :] = rest[:, :128]
    scratch[pl.ds(7, devices, stride=8), :] = rest[:, 128:]
    out_ref[...] = (
        scratch[...].reshape(out_ref.shape).astype(jnp.int32).astype(jnp.int16)
    )


def front_kernel(incoming_ref, move_ref, scale_ref, out_ref, scratch):
    devices = out_ref.shape[0]
    scratch[...] = (
        incoming_ref[...].astype(jnp.int32).astype(F32).reshape(scratch.shape)
    )
    plane = [scratch[pl.ds(s, devices, stride=8), :] for s in range(8)]
    codes = jnp.where(iota(plane[7].shape, 1) >= CODES, plane[7], 0.0)
    scales = mm_hot(steps_of(codes), scale_ref[...])
    plane = [plane[s] * scales[:, 128 * s : 128 * s + 128] for s in range(8)]
    main = split3(jnp.concatenate(plane[:CAP], axis=0))
    rest = split3(
        jnp.concatenate(
            [plane[6 + s // 4][:, 32 * (s % 4) : 32 * (s % 4) + 32] for s in range(CAP)],
            axis=0,
        )
    )
    move = move_ref[...]
    main = mm(move, main[0]) + mm(move, main[1]) + mm(move, main[2])
    rest = mm(move, rest[0]) + mm(move, rest[1]) + mm(move, rest[2])
    out_ref[:, 0:128] = main[:devices]
    out_ref[:, 128:256] = main[devices:]
    out_ref[:, 256:384] = jnp.concatenate(
        [rest[:devices], rest[devices:], jnp.zeros((devices, 64), F32)], axis=1
    )


def mm_split(hots, x):
    x0, x1, x2 = split3(x)
    return mm(hots, x0) + mm(hots, x1) + mm(hots, x2)


def pack_kernel(arrived_ref, leaf_land_ref, out_ref):
    land = leaf_land_ref[...]
    rest = arrived_ref[:, 256:384]
    main = mm_split(
        land, jnp.concatenate([arrived_ref[:, 0:128], arrived_ref[:, 128:256]], axis=0)
    )
    rest = mm_split(land, jnp.concatenate([rest[:, 0:32], rest[:, 32:64]], axis=0))
    leaf = main.shape[0]
    out_ref[:leaf] = main
    out_ref[leaf:] = jnp.concatenate(
        [rest[leaf // 4 * k : leaf // 4 * (k + 1)] for k in range(4)], axis=1
    )


def cluster_kernel(arrived_ref, land_ref, forward_ref, transposed_ref):
    first = jnp.transpose(arrived_ref[:, 0:128])
    second = jnp.transpose(arrived_ref[:, 128:256])
    rest = jnp.transpose(arrived_ref[:, 256:384])
    columns = jnp.concatenate(
        [
            jnp.concatenate([first, rest[0:32]], axis=0),
            jnp.concatenate([second, rest[32:64]], axis=0),
        ],
        axis=1,
    )
    joined = mm_hot(columns, land_ref[...])
    forward_ref[...] = joined[:HALF]
    transposed_ref[...] = joined[HALF:]


def mm_full(a, b, dims=NN):
    a0, a1, a2 = a
    b0, b1, b2 = b
    small = mm(a2, b0, dims) + mm(a1, b1, dims) + mm(a0, b2, dims)
    return (small + (mm(a1, b0, dims) + mm(a0, b1, dims))) + mm(a0, b0, dims)


def mm_hot(a, b):
    a0, a1, a2 = split3(a)
    return mm(a0, b) + mm(a1, b) + mm(a2, b)


def small_solve(p, rows):
    n = len(rows)
    p, rows, w, scaled = dict(p), list(rows), {}, []
    for i in range(0, n, 2):
        j = i + 1
        a, h, c = p[i, i], p[i, j], p[j, j]
        r = 1.0 / (a * c - h * h)
        aa, hh, cc = c * r, -(h * r), a * r
        later = range(j + 1, n)
        for m in later:
            w[i, m] = aa * p[i, m] + hh * p[j, m]
            w[j, m] = hh * p[i, m] + cc * p[j, m]
        for m in later:
            for q in range(m, n):
                p[m, q] = p[m, q] - (p[i, m] * w[i, q] + p[j, m] * w[j, q])
        for m in later:
            rows[m] = rows[m] - (w[i, m] * rows[i] + w[j, m] * rows[j])
        scaled.append(aa * rows[i] + hh * rows[j])
        scaled.append(hh * rows[i] + cc * rows[j])
    for i in range(n - 4, -1, -2):
        for q in (i, i + 1):
            for m in range(i + 2, n, 2):
                scaled[q] = scaled[q] - (w[q, m] * scaled[m] + w[q, m + 1] * scaled[m + 1])
    return scaled


def inverse(matrix):
    n, b = matrix.shape[0], 8
    a = [matrix[b * i : b * i + b] for i in range(n // b)]
    shape = a[0].shape
    sub, lane = iota(shape, 0), iota(shape, 1)
    lower, solved = [], []

    def spread(x):
        return jnp.broadcast_to(x, shape)

    for g in range(n // b):
        k = b * g
        rows = [spread(a[g][q : q + 1, :]) for q in range(b)]
        p = {
            (q, r): spread(rows[q][:, k + r : k + r + 1])
            for q in range(b)
            for r in range(q, b)
        }
        inside = jnp.logical_and(lane >= k, lane < k + b)
        rows = [
            jnp.where(inside, jnp.where(lane == k + q, 1.0, 0.0), rows[q])
            for q in range(b)
        ]
        new = small_solve(p, rows)
        left, picked = rows[0], new[0]
        for q in range(1, b):
            left = jnp.where(sub == q, rows[q], left)
            picked = jnp.where(sub == q, new[q], picked)
        lower.append(jnp.where(lane < k + b, left, 0.0))
        solved.append(jnp.where(lane < k + b, picked, 0.0))
        for i in range(g + 1, n // b):
            terms = [spread(a[i][:, k + q : k + q + 1]) * new[q] for q in range(b)]
            while len(terms) > 1:
                terms = [terms[t] + terms[t + 1] for t in range(0, len(terms), 2)]
            a[i] = jnp.where(inside, 0.0, a[i]) - terms[0]
    lower = jnp.transpose(jnp.concatenate(lower, axis=0))
    return mm_full(split3(lower), split3(jnp.concatenate(solved, axis=0)))


def leaf_kernel(spread_ref, order_ref, interp_ref):
    columns = spread_ref.shape[0]
    leaf, rank = interp_ref.shape
    quarter = leaf // 4
    rest = [spread_ref[c, leaf:, :] for c in range(columns)]
    rest = jnp.concatenate(
        [
            jnp.concatenate([x[:, 32 * k : 32 * k + 32] for x in rest], axis=1)
            for k in range(4)
        ],
        axis=0,
    )
    rows = split3(
        jnp.concatenate([spread_ref[c, :leaf, :] for c in range(columns)] + [rest], axis=1)
    )
    pivots = [part[:rank] for part in rows]
    others = [part[rank:] for part in rows]
    eye = jnp.where(iota((rank, rank), 0) == iota((rank, rank), 1), 1.0, 0.0)
    gram = mm_full(pivots, pivots, NT) * (1.0 / (2.0 * K)) + eye
    cross = mm_full(others, pivots, NT) * (1.0 / (2.0 * K))
    chosen = order_ref[:, :rank].astype(F32)
    cross = split3(mm_split(order_ref[:, rank:], cross) - chosen)
    interp_ref[...] = chosen + mm_full(cross, split3(inverse(gram)))


def call(kernel, outs, *args, scratch=(), smem=(), hbm=(), flops=1_000_000):
    spec = [
        pl.BlockSpec(
            memory_space=pltpu.SMEM if i in smem else pltpu.HBM if i in hbm else pltpu.VMEM
        )
        for i in range(len(args))
    ]
    return pl.pallas_call(
        kernel,
        out_shape=outs,
        in_specs=spec,
        out_specs=jax.tree.map(lambda _: pl.BlockSpec(memory_space=pltpu.VMEM), outs),
        scratch_shapes=scratch,
        compiler_params=pltpu.CompilerParams(vmem_limit_bytes=48 * 2**20),
        cost_estimate=pl.CostEstimate(
            flops=flops, bytes_accessed=1_000_000, transcendentals=0
        ),
    )(*args)


def per_device(right_sample, left_sample, updates, pattern, targets, cluster_pos, pivots):
    devices = lax.axis_size("rows")
    local_rows, width = right_sample.shape
    block = updates.shape[1]
    shape = jax.ShapeDtypeStruct

    def exchange(x):
        return lax.all_to_all(x, "rows", split_axis=0, concat_axis=0, tiled=True)

    message, front_order = call(
        request_kernel,
        [shape((devices, 128), jnp.int32), shape((devices, 128), jnp.int32)],
        pltpu.with_memory_space_constraint(targets, pltpu.HBM),
        pltpu.with_memory_space_constraint(cluster_pos.reshape(1, local_rows), pltpu.HBM),
        hbm=(0, 1),
        scratch=[
            pltpu.VMEM((1, block), jnp.int32),
            pltpu.VMEM((1, local_rows), jnp.int32),
            pltpu.SemaphoreType.DMA((2,)),
        ],
    )
    received = exchange(message)
    slots, member, rank, masked = call(
        tile_prep_kernel,
        [
            shape((CAP * devices, block), BF16),
            shape((devices, block), BF16),
            shape((8, block), F32),
            shape((block, block), BF16),
        ],
        targets,
        pattern[0],
        updates[0],
        smem=(1,),
    )
    reply = call(
        reply_kernel,
        shape((devices, 8, 128), BF16),
        received,
        right_sample.T,
        left_sample.T,
        scratch=[pltpu.VMEM((devices * 8, 128), F32)],
    )
    fetched = exchange(reply)
    move, land, leaf_land, scale, order = call(
        front_prep_kernel,
        [
            shape((2 * devices, CAP * devices), BF16),
            shape((2 * devices, local_rows), BF16),
            shape((local_rows, 2 * devices), BF16),
            shape((128, 1024), BF16),
            shape((local_rows, local_rows), BF16),
        ],
        received,
        front_order,
        pivots,
    )
    outgoing = call(
        tile_kernel,
        shape((devices, 8, 128), jnp.int16),
        fetched,
        slots,
        member,
        rank,
        masked,
        scratch=[pltpu.VMEM((devices * 8, 128), F32)],
    )
    incoming = exchange(outgoing)
    moved = call(
        front_kernel,
        shape((devices, 384), F32),
        incoming,
        move,
        scale,
        scratch=[pltpu.VMEM((devices * 8, 128), F32)],
    )
    arrived = exchange(moved)
    packed = call(
        pack_kernel, shape((local_rows * 5 // 4, 128), F32), arrived, leaf_land
    )
    columns = lax.axis_size("cols")
    spread = lax.all_to_all(
        jnp.broadcast_to(packed[None], (columns,) + packed.shape),
        "cols",
        split_axis=0,
        concat_axis=0,
        tiled=True,
    )
    forward, transposed = call(
        cluster_kernel,
        [shape((width, local_rows), F32), shape((width, local_rows), F32)],
        arrived,
        land,
    )
    interp = call(
        leaf_kernel, shape((local_rows, pivots.shape[1]), F32), spread, order
    )
    return forward.T, transposed.T, interp


def solution(mesh):
    return jax.shard_map(
        per_device,
        mesh=mesh,
        in_specs=(
            P("rows", "cols"),
            P("rows", "cols"),
            P("rows", None, None),
            P("rows", None, None),
            P("rows", None),
            P("rows"),
            P("rows", None),
        ),
        out_specs=(P("rows", "cols"), P("rows", "cols"), P("rows", None)),
        check_vma=False,
    )
```

```python
import jax
import jax.numpy as jnp
from jax import lax
from jax.experimental import pallas as pl
from jax.experimental.pallas import tpu as pltpu
from jax.sharding import PartitionSpec as P

K = 320
CAP = 6
HALF = 80
CODES = 64
LOG2 = 0.6931471805599453
F32 = jnp.float32
BF16 = jnp.bfloat16
NT = (((1,), (1,)), ((), ()))
NN = (((1,), (0,)), ((), ()))


def mm(a, b, dims=NN):
    return lax.dot_general(a, b, dims, preferred_element_type=F32)


def iota(shape, dim):
    return lax.broadcasted_iota(jnp.int32, shape, dim)


def split3(x):
    hi = x.astype(BF16)
    rest = x - hi.astype(F32)
    mid = rest.astype(BF16)
    low = (rest - mid.astype(F32)).astype(BF16)
    return hi, mid, low


def hot(mask):
    return jnp.where(mask, 1.0, 0.0).astype(BF16)


def ranks(keys, devices):
    n = keys.shape[1]
    member = keys == iota((devices, n), 0)
    ahead = hot(iota((n, n), 0) < iota((n, n), 1))
    return member, mm(hot(member), ahead)


def pick(member, rank, slot, values):
    chosen = jnp.where(jnp.logical_and(member, rank == float(slot)), values, 0.0)
    return jnp.sum(chosen, axis=1, keepdims=True)


def request_kernel(targets_hbm, pos_hbm, msg_ref, targets_ref, pos_ref, arrivals):
    devices = msg_ref.shape[0]
    first = pltpu.make_async_copy(targets_hbm, targets_ref, arrivals.at[0])
    second = pltpu.make_async_copy(pos_hbm, pos_ref, arrivals.at[1])
    first.start()
    second.start()
    first.wait()
    second.wait()
    lanes = iota((devices, 128), 1)
    wanted = targets_ref[...]
    member, rank = ranks(wanted >> 8, devices)
    local = ((wanted & 255) + 1).astype(F32)
    msg = jnp.zeros((devices, 128), F32)
    for slot in range(CAP):
        msg = jnp.where(lanes == slot, pick(member, rank, slot, local) - 1.0, msg)
    pos = pos_ref[...]
    member, rank = ranks(pos >> 8, devices)
    landing = (pos & 255).astype(F32)
    for slot in range(2):
        msg = jnp.where(lanes == CAP + slot, pick(member, rank, slot, landing), msg)
    msg_ref[...] = msg.astype(jnp.int32)


def prep_kernel(
    targets_ref,
    pattern_ref,
    updates_ref,
    pos_ref,
    pivots_ref,
    slots_ref,
    member_ref,
    rank_ref,
    masked_ref,
    rows_ref,
    order_ref,
    index_ref,
    scale_ref,
):
    devices = member_ref.shape[0]
    member, rank = ranks(targets_ref[...] >> 8, devices)
    member_ref[...] = hot(member)
    rank_ref[...] = jnp.broadcast_to(
        jnp.sum(jnp.where(member, rank, 0.0), axis=0, keepdims=True), rank_ref.shape
    )
    for slot in range(CAP):
        slots_ref[slot * devices : (slot + 1) * devices, :] = hot(
            jnp.logical_and(member, rank == float(slot))
        )
    for a in range(4):
        for b in range(4):
            part = updates_ref[a * 128 : (a + 1) * 128, b * 128 : (b + 1) * 128]
            keep = pattern_ref[a, b] != 0
            masked_ref[a * 128 : (a + 1) * 128, b * 128 : (b + 1) * 128] = jnp.where(
                keep, part, jnp.zeros_like(part)
            )
    pos = pos_ref[...]
    member, rank = ranks(pos >> 8, devices)
    here = iota(pos.shape, 1).astype(F32)
    place, lane = iota((128, 128), 0), iota((128, 128), 1)
    rows = jnp.zeros(rows_ref.shape, F32)
    for slot in range(2):
        rows = jnp.where(lane == slot, pick(member, rank, slot, here), rows)
    rows_ref[...] = rows.astype(jnp.int32)
    leaf, count = order_ref.shape[0], pivots_ref.shape[1]
    pivot = iota((leaf, count), 0) == pivots_ref[...]
    other = 1.0 - jnp.sum(jnp.where(pivot, 1.0, 0.0), axis=1, keepdims=True)
    other = jnp.broadcast_to(other, (leaf, leaf - count))
    ahead = mm(hot(iota((leaf, leaf), 1) < iota((leaf, leaf), 0)), other.astype(BF16))
    order_ref[:, :count] = hot(pivot)
    order_ref[:, count:] = hot(
        jnp.logical_and(other > 0.5, ahead == iota(ahead.shape, 1).astype(F32))
    )
    place_of = jnp.where(order_ref[...] > 0.5, iota((leaf, leaf), 1).astype(F32), 0.0)
    index_ref[...] = jnp.broadcast_to(
        jnp.sum(place_of, axis=1, keepdims=True), index_ref.shape
    )
    for s in range(CAP):
        scale_ref[:, 128 * s : 128 * s + 128] = hot(
            place == CODES + s + jnp.where(lane >= HALF, 8, 0)
        )
    for s in (6, 7):
        scale_ref[:, 128 * s : 128 * s + 128] = hot(
            place == CODES + 8 + 4 * (s - 6) + (lane >> 5)
        )


def reply_kernel(recv_ref, right_ref, left_ref, out_ref, scratch):
    devices = recv_ref.shape[0]
    samples = jnp.concatenate([right_ref[...], left_ref[...]], axis=0)
    places = iota((devices, samples.shape[1]), 1)
    chosen = jnp.concatenate(
        [hot(recv_ref[:, s : s + 1] == places) for s in range(CAP)], axis=0
    )
    rows = mm(chosen, samples, NT)
    part = [rows[s * devices : (s + 1) * devices] for s in range(CAP)]
    for s in range(CAP):
        scratch[pl.ds(s, devices, stride=8), :] = part[s][:, :128]
    scratch[pl.ds(6, devices, stride=8), :] = jnp.concatenate(
        [part[s][:, 128:160] for s in range(4)], axis=1
    )
    scratch[pl.ds(7, devices, stride=8), :] = jnp.concatenate(
        [part[4][:, 128:160], part[5][:, 128:160], jnp.zeros((devices, 64), F32)], axis=1
    )
    out_ref[...] = scratch[...].reshape(out_ref.shape).astype(BF16)


def steps_of(code):
    return jnp.exp(code * (LOG2 / 256.0)) * (1.0 / 32600.0)


def coded(x):
    peak = jnp.maximum(jnp.max(jnp.abs(x), axis=0, keepdims=True), 1e-32)
    code = jnp.ceil(jnp.log(peak) * (256.0 / LOG2))
    return jnp.floor(x / steps_of(code) + 0.5), code


def mm_whole(hots, x):
    high = jnp.floor(x * (1.0 / 256.0) + 0.5)
    low = x - 256.0 * high
    return mm(hots, high.astype(BF16), NT) * 256.0 + mm(hots, low.astype(BF16), NT)


def tile_kernel(
    fetched_ref, slots_ref, member_ref, rank_ref, masked_ref, out_ref, scratch
):
    devices, columns = member_ref.shape
    scratch[...] = fetched_ref[...].astype(F32).reshape(scratch.shape)
    across = [
        jnp.transpose(scratch[pl.ds(s, devices, stride=8), :]).astype(BF16)
        for s in range(8)
    ]
    slots, member, rank = slots_ref[...], member_ref[...], rank_ref[0:1, :]
    main = mm(jnp.concatenate(across[:CAP], axis=1), slots)
    rest = mm(jnp.concatenate(across[CAP:], axis=0), member)
    tail = jnp.zeros((32, columns), F32)
    for s in range(CAP):
        tail = jnp.where(rank == float(s), rest[32 * s : 32 * s + 32], tail)
    gathered = jnp.concatenate([main, tail], axis=0).astype(BF16)
    masked = masked_ref[...]
    forward, forward_code = coded(mm(gathered[:HALF], masked, NT))
    transposed, transposed_code = coded(mm(gathered[HALF:], masked, NN))
    tail = transposed[128 - HALF :]
    row = iota((8, columns), 0).astype(F32)
    rest = jnp.concatenate(
        [jnp.where(rank == float(s), tail, 0.0) for s in range(CAP)]
        + [
            jnp.where(rank == row, forward_code, 0.0),
            jnp.where(rank == row, transposed_code, 0.0),
            jnp.zeros((48, columns), F32),
        ],
        axis=0,
    )
    main = mm_whole(slots, jnp.concatenate([forward, transposed[: 128 - HALF]], axis=0))
    rest = mm_whole(member, rest)
    for s in range(CAP):
        scratch[pl.ds(s, devices, stride=8), :] = main[s * devices : (s + 1) * devices]
    scratch[pl.ds(6, devices, stride=8), :] = rest[:, :128]
    scratch[pl.ds(7, devices, stride=8), :] = rest[:, 128:]
    out_ref[...] = (
        scratch[...].reshape(out_ref.shape).astype(jnp.int32).astype(jnp.int16)
    )


def front_kernel(incoming_ref, recv_ref, rows_ref, scale_ref, out_ref, scratch):
    devices = out_ref.shape[0]
    across = jnp.transpose(recv_ref[...].astype(F32)).astype(jnp.int32)
    move = jnp.concatenate(
        [
            jnp.concatenate(
                [
                    hot(rows_ref[:, g : g + 1] == across[s : s + 1, :])
                    for s in range(CAP)
                ],
                axis=1,
            )
            for g in range(2)
        ],
        axis=0,
    )
    scratch[...] = (
        incoming_ref[...].astype(jnp.int32).astype(F32).reshape(scratch.shape)
    )
    plane = [scratch[pl.ds(s, devices, stride=8), :] for s in range(8)]
    codes = jnp.where(iota(plane[7].shape, 1) >= CODES, plane[7], 0.0)
    scales = mm_hot(steps_of(codes), scale_ref[...])
    plane = [plane[s] * scales[:, 128 * s : 128 * s + 128] for s in range(8)]
    main = split3(jnp.concatenate(plane[:CAP], axis=0))
    rest = split3(
        jnp.concatenate(
            [plane[6 + s // 4][:, 32 * (s % 4) : 32 * (s % 4) + 32] for s in range(CAP)],
            axis=0,
        )
    )
    main = mm(move, main[0]) + mm(move, main[1]) + mm(move, main[2])
    rest = mm(move, rest[0]) + mm(move, rest[1]) + mm(move, rest[2])
    out_ref[:, 0:128] = main[:devices]
    out_ref[:, 128:256] = main[devices:]
    out_ref[:, 256:384] = jnp.concatenate(
        [rest[:devices], rest[devices:], jnp.zeros((devices, 64), F32)], axis=1
    )


def mm_split(hots, x):
    x0, x1, x2 = split3(x)
    return mm(hots, x0) + mm(hots, x1) + mm(hots, x2)


def pack_kernel(arrived_ref, recv_ref, index_ref, out_ref):
    leaf = index_ref.shape[0]
    across = jnp.transpose(recv_ref[...].astype(F32))
    landing = jnp.concatenate([across[CAP : CAP + 1], across[CAP + 1 : CAP + 2]], axis=1)
    row = iota((leaf, landing.shape[1]), 0).astype(F32)
    index = jnp.sum(
        jnp.where(row == landing, index_ref[...], 0.0), axis=0, keepdims=True
    )
    land = hot(row == index)
    rest = arrived_ref[:, 256:384]
    main = mm_split(
        land, jnp.concatenate([arrived_ref[:, 0:128], arrived_ref[:, 128:256]], axis=0)
    )
    rest = mm_split(land, jnp.concatenate([rest[:, 0:32], rest[:, 32:64]], axis=0))
    rest = jnp.concatenate(
        [rest[leaf // 4 * k : leaf // 4 * (k + 1)] for k in range(4)], axis=1
    )
    for c in range(out_ref.shape[0]):
        out_ref[c, :leaf] = main
        out_ref[c, leaf:] = rest


def cluster_rows(arrived_ref, recv_ref, forward_ref, transposed_ref):
    devices, leaf = arrived_ref.shape[0], forward_ref.shape[1]
    land = jnp.concatenate(
        [
            hot(recv_ref[:, CAP + g : CAP + g + 1] == iota((devices, leaf), 1))
            for g in range(2)
        ],
        axis=0,
    )
    first = jnp.transpose(arrived_ref[:, 0:128])
    second = jnp.transpose(arrived_ref[:, 128:256])
    rest = jnp.transpose(arrived_ref[:, 256:384])
    columns = jnp.concatenate(
        [
            jnp.concatenate([first, rest[0:32]], axis=0),
            jnp.concatenate([second, rest[32:64]], axis=0),
        ],
        axis=1,
    )
    joined = mm_hot(columns, land)
    forward_ref[...] = joined[:HALF]
    transposed_ref[...] = joined[HALF:]


def mm_full(a, b, dims=NN):
    a0, a1, a2 = a
    b0, b1, b2 = b
    small = mm(a2, b0, dims) + mm(a1, b1, dims) + mm(a0, b2, dims)
    return (small + (mm(a1, b0, dims) + mm(a0, b1, dims))) + mm(a0, b0, dims)


def mm_hot(a, b):
    a0, a1, a2 = split3(a)
    return mm(a0, b) + mm(a1, b) + mm(a2, b)


def small_solve(p, rows):
    n = len(rows)
    p, rows, w, scaled = dict(p), list(rows), {}, []
    for i in range(0, n, 2):
        j = i + 1
        a, h, c = p[i, i], p[i, j], p[j, j]
        r = 1.0 / (a * c - h * h)
        aa, hh, cc = c * r, -(h * r), a * r
        later = range(j + 1, n)
        for m in later:
            w[i, m] = aa * p[i, m] + hh * p[j, m]
            w[j, m] = hh * p[i, m] + cc * p[j, m]
        for m in later:
            for q in range(m, n):
                p[m, q] = p[m, q] - (p[i, m] * w[i, q] + p[j, m] * w[j, q])
        for m in later:
            rows[m] = rows[m] - (w[i, m] * rows[i] + w[j, m] * rows[j])
        scaled.append(aa * rows[i] + hh * rows[j])
        scaled.append(hh * rows[i] + cc * rows[j])
    for i in range(n - 4, -1, -2):
        for q in (i, i + 1):
            for m in range(i + 2, n, 2):
                scaled[q] = scaled[q] - (w[q, m] * scaled[m] + w[q, m + 1] * scaled[m + 1])
    return scaled


def inverse(matrix):
    n, b = matrix.shape[0], 8
    a = [matrix[b * i : b * i + b] for i in range(n // b)]
    shape = a[0].shape
    sub, lane = iota(shape, 0), iota(shape, 1)
    lower, solved = [], []

    def spread(x):
        return jnp.broadcast_to(x, shape)

    for g in range(n // b):
        k = b * g
        rows = [spread(a[g][q : q + 1, :]) for q in range(b)]
        p = {
            (q, r): spread(rows[q][:, k + r : k + r + 1])
            for q in range(b)
            for r in range(q, b)
        }
        inside = jnp.logical_and(lane >= k, lane < k + b)
        rows = [
            jnp.where(inside, jnp.where(lane == k + q, 1.0, 0.0), rows[q])
            for q in range(b)
        ]
        new = small_solve(p, rows)
        left, picked = rows[0], new[0]
        for q in range(1, b):
            left = jnp.where(sub == q, rows[q], left)
            picked = jnp.where(sub == q, new[q], picked)
        lower.append(jnp.where(lane < k + b, left, 0.0))
        solved.append(jnp.where(lane < k + b, picked, 0.0))
        for i in range(g + 1, n // b):
            terms = [spread(a[i][:, k + q : k + q + 1]) * new[q] for q in range(b)]
            while len(terms) > 1:
                terms = [terms[t] + terms[t + 1] for t in range(0, len(terms), 2)]
            a[i] = jnp.where(inside, 0.0, a[i]) - terms[0]
    lower = jnp.transpose(jnp.concatenate(lower, axis=0))
    return mm_full(split3(lower), split3(jnp.concatenate(solved, axis=0)))


def leaf_kernel(
    spread_ref,
    order_ref,
    arrived_ref,
    recv_ref,
    interp_ref,
    forward_ref,
    transposed_ref,
):
    cluster_rows(arrived_ref, recv_ref, forward_ref, transposed_ref)
    columns = spread_ref.shape[0]
    leaf, rank = interp_ref.shape
    quarter = leaf // 4
    rest = [spread_ref[c, leaf:, :] for c in range(columns)]
    rest = jnp.concatenate(
        [
            jnp.concatenate([x[:, 32 * k : 32 * k + 32] for x in rest], axis=1)
            for k in range(4)
        ],
        axis=0,
    )
    rows = split3(
        jnp.concatenate([spread_ref[c, :leaf, :] for c in range(columns)] + [rest], axis=1)
    )
    pivots = [part[:rank] for part in rows]
    others = [part[rank:] for part in rows]
    eye = jnp.where(iota((rank, rank), 0) == iota((rank, rank), 1), 1.0, 0.0)
    gram = mm_full(pivots, pivots, NT) * (1.0 / (2.0 * K)) + eye
    cross = mm_full(others, pivots, NT) * (1.0 / (2.0 * K))
    chosen = order_ref[:, :rank].astype(F32)
    cross = split3(mm_split(order_ref[:, rank:], cross) - chosen)
    interp_ref[...] = chosen + mm_full(cross, split3(inverse(gram)))


def call(kernel, outs, *args, scratch=(), smem=(), hbm=(), flops=1_000_000):
    spec = [
        pl.BlockSpec(
            memory_space=pltpu.SMEM if i in smem else pltpu.HBM if i in hbm else pltpu.VMEM
        )
        for i in range(len(args))
    ]
    return pl.pallas_call(
        kernel,
        out_shape=outs,
        in_specs=spec,
        out_specs=jax.tree.map(lambda _: pl.BlockSpec(memory_space=pltpu.VMEM), outs),
        scratch_shapes=scratch,
        compiler_params=pltpu.CompilerParams(vmem_limit_bytes=48 * 2**20),
        cost_estimate=pl.CostEstimate(
            flops=flops, bytes_accessed=1_000_000, transcendentals=0
        ),
    )(*args)


def per_device(right_sample, left_sample, updates, pattern, targets, cluster_pos, pivots):
    devices = lax.axis_size("rows")
    local_rows, width = right_sample.shape
    block = updates.shape[1]
    shape = jax.ShapeDtypeStruct

    def exchange(x):
        return lax.all_to_all(x, "rows", split_axis=0, concat_axis=0, tiled=True)

    positions = cluster_pos.reshape(1, local_rows)
    message = call(
        request_kernel,
        shape((devices, 128), jnp.int32),
        pltpu.with_memory_space_constraint(targets, pltpu.HBM),
        pltpu.with_memory_space_constraint(positions, pltpu.HBM),
        hbm=(0, 1),
        scratch=[
            pltpu.VMEM((1, block), jnp.int32),
            pltpu.VMEM((1, local_rows), jnp.int32),
            pltpu.SemaphoreType.DMA((2,)),
        ],
    )
    received = exchange(message)
    prepared = call(
        prep_kernel,
        [
            shape((CAP * devices, block), BF16),
            shape((devices, block), BF16),
            shape((8, block), F32),
            shape((block, block), BF16),
            shape((devices, 128), jnp.int32),
            shape((local_rows, local_rows), BF16),
            shape((local_rows, local_rows), F32),
            shape((128, 1024), BF16),
        ],
        targets,
        pattern[0],
        updates[0],
        positions,
        pivots,
        smem=(1,),
    )
    received, *prepared = lax.optimization_barrier((received, *prepared))
    slots, member, rank, masked, rows, order, index, scale = prepared
    reply = call(
        reply_kernel,
        shape((devices, 8, 128), BF16),
        received,
        right_sample.T,
        left_sample.T,
        scratch=[pltpu.VMEM((devices * 8, 128), F32)],
    )
    fetched = exchange(reply)
    outgoing = call(
        tile_kernel,
        shape((devices, 8, 128), jnp.int16),
        fetched,
        slots,
        member,
        rank,
        masked,
        scratch=[pltpu.VMEM((devices * 8, 128), F32)],
    )
    incoming = exchange(outgoing)
    moved = call(
        front_kernel,
        shape((devices, 384), F32),
        incoming,
        received,
        rows,
        scale,
        scratch=[pltpu.VMEM((devices * 8, 128), F32)],
    )
    arrived = exchange(moved)
    columns = lax.axis_size("cols")
    packed = call(
        pack_kernel,
        shape((columns, local_rows * 5 // 4, 128), F32),
        arrived,
        received,
        index,
    )
    spread = lax.all_to_all(packed, "cols", split_axis=0, concat_axis=0, tiled=True)
    interp, forward, transposed = call(
        leaf_kernel,
        [
            shape((local_rows, pivots.shape[1]), F32),
            shape((width, local_rows), F32),
            shape((width, local_rows), F32),
        ],
        spread,
        order,
        arrived,
        received,
    )
    return forward.T, transposed.T, interp


def solution(mesh):
    return jax.shard_map(
        per_device,
        mesh=mesh,
        in_specs=(
            P("rows", "cols"),
            P("rows", "cols"),
            P("rows", None, None),
            P("rows", None, None),
            P("rows", None),
            P("rows"),
            P("rows", None),
        ),
        out_specs=(P("rows", "cols"), P("rows", "cols"), P("rows", None)),
        check_vma=False,
    )
```

```python
import jax
import jax.numpy as jnp
from jax import lax
from jax.experimental import pallas as pl
from jax.experimental.pallas import tpu as pltpu
from jax.sharding import PartitionSpec as P

K = 320
CAP = 6
HALF = 80
CODES = 64
LOG2 = 0.6931471805599453
F32 = jnp.float32
BF16 = jnp.bfloat16
NT = (((1,), (1,)), ((), ()))
NN = (((1,), (0,)), ((), ()))


def mm(a, b, dims=NN):
    return lax.dot_general(a, b, dims, preferred_element_type=F32)


def iota(shape, dim):
    return lax.broadcasted_iota(jnp.int32, shape, dim)


def split3(x):
    hi = x.astype(BF16)
    rest = x - hi.astype(F32)
    mid = rest.astype(BF16)
    low = (rest - mid.astype(F32)).astype(BF16)
    return hi, mid, low


def hot(mask):
    return jnp.where(mask, 1.0, 0.0).astype(BF16)


def ranks(keys, devices):
    n = keys.shape[1]
    member = keys == iota((devices, n), 0)
    ahead = hot(iota((n, n), 0) < iota((n, n), 1))
    return member, mm(hot(member), ahead)


def pick(member, rank, slot, values):
    chosen = jnp.where(jnp.logical_and(member, rank == float(slot)), values, 0.0)
    return jnp.sum(chosen, axis=1, keepdims=True)


def request_kernel(targets_hbm, pos_hbm, msg_ref, targets_ref, pos_ref, arrivals):
    devices = msg_ref.shape[0]
    first = pltpu.make_async_copy(targets_hbm, targets_ref, arrivals.at[0])
    second = pltpu.make_async_copy(pos_hbm, pos_ref, arrivals.at[1])
    first.start()
    second.start()
    first.wait()
    second.wait()
    lanes = iota((devices, 128), 1)
    wanted = targets_ref[...]
    member, rank = ranks(wanted >> 8, devices)
    local = ((wanted & 255) + 1).astype(F32)
    msg = jnp.zeros((devices, 128), F32)
    for slot in range(CAP):
        msg = jnp.where(lanes == slot, pick(member, rank, slot, local) - 1.0, msg)
    pos = pos_ref[...]
    member, rank = ranks(pos >> 8, devices)
    landing = (pos & 255).astype(F32)
    for slot in range(2):
        msg = jnp.where(lanes == CAP + slot, pick(member, rank, slot, landing), msg)
    msg_ref[...] = msg.astype(jnp.int32)


def prep_kernel(
    targets_ref,
    pattern_ref,
    updates_ref,
    pos_ref,
    pivots_ref,
    slots_ref,
    member_ref,
    rank_ref,
    masked_ref,
    rows_ref,
    order_ref,
    index_ref,
    scale_ref,
    leaf_scale_ref,
):
    devices = member_ref.shape[0]
    member, rank = ranks(targets_ref[...] >> 8, devices)
    member_ref[...] = hot(member)
    rank_ref[...] = jnp.broadcast_to(
        jnp.sum(jnp.where(member, rank, 0.0), axis=0, keepdims=True), rank_ref.shape
    )
    for slot in range(CAP):
        slots_ref[slot * devices : (slot + 1) * devices, :] = hot(
            jnp.logical_and(member, rank == float(slot))
        )
    for a in range(4):
        for b in range(4):
            part = updates_ref[a * 128 : (a + 1) * 128, b * 128 : (b + 1) * 128]
            keep = pattern_ref[a, b] != 0
            masked_ref[a * 128 : (a + 1) * 128, b * 128 : (b + 1) * 128] = jnp.where(
                keep, part, jnp.zeros_like(part)
            )
    pos = pos_ref[...]
    member, rank = ranks(pos >> 8, devices)
    here = iota(pos.shape, 1).astype(F32)
    place, lane = iota((128, 128), 0), iota((128, 128), 1)
    rows = jnp.zeros(rows_ref.shape, F32)
    for slot in range(2):
        rows = jnp.where(lane == slot, pick(member, rank, slot, here), rows)
    rows_ref[...] = rows.astype(jnp.int32)
    leaf, count = order_ref.shape[0], pivots_ref.shape[1]
    pivot = iota((leaf, count), 0) == pivots_ref[...]
    other = 1.0 - jnp.sum(jnp.where(pivot, 1.0, 0.0), axis=1, keepdims=True)
    other = jnp.broadcast_to(other, (leaf, leaf - count))
    ahead = mm(hot(iota((leaf, leaf), 1) < iota((leaf, leaf), 0)), other.astype(BF16))
    order_ref[:, :count] = hot(pivot)
    order_ref[:, count:] = hot(
        jnp.logical_and(other > 0.5, ahead == iota(ahead.shape, 1).astype(F32))
    )
    place_of = jnp.where(order_ref[...] > 0.5, iota((leaf, leaf), 1).astype(F32), 0.0)
    index_ref[...] = jnp.broadcast_to(
        jnp.sum(place_of, axis=1, keepdims=True), index_ref.shape
    )
    for s in range(CAP):
        scale_ref[:, 128 * s : 128 * s + 128] = hot(
            place == CODES + s + jnp.where(lane >= HALF, 8, 0)
        )
    for s in (6, 7):
        scale_ref[:, 128 * s : 128 * s + 128] = hot(
            place == CODES + 8 + 4 * (s - 6) + (lane >> 5)
        )
    for c in range(4):
        leaf_scale_ref[:, 128 * c : 128 * c + 128] = hot(
            place == 32 * c + jnp.where(lane >= HALF, 1, 0)
        )
    leaf_scale_ref[:, 512:640] = hot(place == 32 * (lane >> 5) + 1)


def reply_kernel(recv_ref, right_ref, left_ref, out_ref, scratch):
    devices = recv_ref.shape[0]
    samples = jnp.concatenate([right_ref[...], left_ref[...]], axis=0)
    places = iota((devices, samples.shape[1]), 1)
    chosen = jnp.concatenate(
        [hot(recv_ref[:, s : s + 1] == places) for s in range(CAP)], axis=0
    )
    rows = mm(chosen, samples, NT)
    part = [rows[s * devices : (s + 1) * devices] for s in range(CAP)]
    for s in range(CAP):
        scratch[pl.ds(s, devices, stride=8), :] = part[s][:, :128]
    scratch[pl.ds(6, devices, stride=8), :] = jnp.concatenate(
        [part[s][:, 128:160] for s in range(4)], axis=1
    )
    scratch[pl.ds(7, devices, stride=8), :] = jnp.concatenate(
        [part[4][:, 128:160], part[5][:, 128:160], jnp.zeros((devices, 64), F32)], axis=1
    )
    out_ref[...] = scratch[...].reshape(out_ref.shape).astype(BF16)


def steps_of(code):
    return jnp.exp(code * (LOG2 / 256.0)) * (1.0 / 32600.0)


def code_of(peak):
    return jnp.ceil(jnp.log(jnp.maximum(peak, 1e-32)) * (256.0 / LOG2))


def coded(x):
    code = code_of(jnp.max(jnp.abs(x), axis=0, keepdims=True))
    return jnp.floor(x / steps_of(code) + 0.5), code


def halves(x):
    high = jnp.floor(x * (1.0 / 256.0) + 0.5)
    low = x - 256.0 * high
    return high.astype(BF16), low.astype(BF16)


def mm_whole(hots, x, dims=NT):
    high, low = halves(x)
    return mm(hots, high, dims) * 256.0 + mm(hots, low, dims)


def tile_kernel(
    fetched_ref, slots_ref, member_ref, rank_ref, masked_ref, out_ref, scratch
):
    devices, columns = member_ref.shape
    scratch[...] = fetched_ref[...].astype(F32).reshape(scratch.shape)
    across = [
        jnp.transpose(scratch[pl.ds(s, devices, stride=8), :]).astype(BF16)
        for s in range(8)
    ]
    slots, member, rank = slots_ref[...], member_ref[...], rank_ref[0:1, :]
    main = mm(jnp.concatenate(across[:CAP], axis=1), slots)
    rest = mm(jnp.concatenate(across[CAP:], axis=0), member)
    tail = jnp.zeros((32, columns), F32)
    for s in range(CAP):
        tail = jnp.where(rank == float(s), rest[32 * s : 32 * s + 32], tail)
    gathered = jnp.concatenate([main, tail], axis=0).astype(BF16)
    masked = masked_ref[...]
    forward, forward_code = coded(mm(gathered[:HALF], masked, NT))
    transposed, transposed_code = coded(mm(gathered[HALF:], masked, NN))
    tail = transposed[128 - HALF :]
    row = iota((8, columns), 0).astype(F32)
    rest = jnp.concatenate(
        [jnp.where(rank == float(s), tail, 0.0) for s in range(CAP)]
        + [
            jnp.where(rank == row, forward_code, 0.0),
            jnp.where(rank == row, transposed_code, 0.0),
            jnp.zeros((48, columns), F32),
        ],
        axis=0,
    )
    main = mm_whole(slots, jnp.concatenate([forward, transposed[: 128 - HALF]], axis=0))
    rest = mm_whole(member, rest)
    for s in range(CAP):
        scratch[pl.ds(s, devices, stride=8), :] = main[s * devices : (s + 1) * devices]
    scratch[pl.ds(6, devices, stride=8), :] = rest[:, :128]
    scratch[pl.ds(7, devices, stride=8), :] = rest[:, 128:]
    out_ref[...] = (
        scratch[...].reshape(out_ref.shape).astype(jnp.int32).astype(jnp.int16)
    )


def front_kernel(incoming_ref, recv_ref, rows_ref, scale_ref, out_ref, scratch, sent):
    devices = recv_ref.shape[0]
    across = jnp.transpose(recv_ref[...].astype(F32)).astype(jnp.int32)
    move = jnp.concatenate(
        [
            jnp.concatenate(
                [
                    hot(rows_ref[:, g : g + 1] == across[s : s + 1, :])
                    for s in range(CAP)
                ],
                axis=1,
            )
            for g in range(2)
        ],
        axis=0,
    )
    scratch[...] = (
        incoming_ref[...].astype(jnp.int32).astype(F32).reshape(scratch.shape)
    )
    plane = [scratch[pl.ds(s, devices, stride=8), :] for s in range(8)]
    codes = jnp.where(iota(plane[7].shape, 1) >= CODES, plane[7], 0.0)
    scales = mm_hot(steps_of(codes), scale_ref[...])
    plane = [plane[s] * scales[:, 128 * s : 128 * s + 128] for s in range(8)]
    main = split3(jnp.concatenate(plane[:CAP], axis=0))
    rest = split3(
        jnp.concatenate(
            [plane[6 + s // 4][:, 32 * (s % 4) : 32 * (s % 4) + 32] for s in range(CAP)],
            axis=0,
        )
    )
    main = mm(move, main[0]) + mm(move, main[1]) + mm(move, main[2])
    rest = mm(move, rest[0]) + mm(move, rest[1]) + mm(move, rest[2])
    lane = iota(main.shape, 1)
    size = jnp.abs(main)
    peaks = [
        jnp.max(jnp.where(lane < HALF, size, 0.0), axis=1, keepdims=True),
        jnp.maximum(
            jnp.max(jnp.where(lane >= HALF, size, 0.0), axis=1, keepdims=True),
            jnp.max(jnp.abs(rest), axis=1, keepdims=True),
        ),
    ]
    codes = [code_of(peak) for peak in peaks]
    steps = [1.0 / steps_of(code) for code in codes]
    main = jnp.floor(main * jnp.where(lane < HALF, steps[0], steps[1]) + 0.5)
    rest = jnp.floor(rest * steps[1] + 0.5)
    rest = jnp.concatenate(
        [
            rest[:devices],
            jnp.zeros((devices, 8), F32),
            rest[devices:],
            jnp.zeros((devices, 56), F32),
        ],
        axis=1,
    )
    lane = iota(rest.shape, 1)
    for g in range(2):
        for h in range(2):
            code = codes[h][g * devices : (g + 1) * devices]
            rest = jnp.where(lane == 40 * g + 32 + h, code, rest)
    sent[pl.ds(0, devices, stride=4), :] = main[:devices]
    sent[pl.ds(1, devices, stride=4), :] = main[devices:]
    sent[pl.ds(2, devices, stride=4), :] = rest
    sent[pl.ds(3, devices, stride=4), :] = jnp.zeros_like(rest)
    out_ref[...] = sent[...].astype(jnp.int32).astype(jnp.int16)


def mm_split(hots, x):
    x0, x1, x2 = split3(x)
    return mm(hots, x0) + mm(hots, x1) + mm(hots, x2)


def pack_kernel(arrived_ref, recv_ref, index_ref, out_ref, plane_ref, scratch):
    leaf, devices = index_ref.shape[0], recv_ref.shape[0]
    scratch[...] = arrived_ref[...].astype(jnp.int32).astype(F32)
    plane = [scratch[pl.ds(r, devices, stride=4), :] for r in range(3)]
    for r in range(3):
        plane_ref[r * devices : (r + 1) * devices, :] = plane[r]
    across = jnp.transpose(recv_ref[...].astype(F32))
    landing = jnp.concatenate([across[CAP : CAP + 1], across[CAP + 1 : CAP + 2]], axis=1)
    row = iota((leaf, landing.shape[1]), 0).astype(F32)
    index = jnp.sum(
        jnp.where(row == landing, index_ref[...], 0.0), axis=0, keepdims=True
    )
    land = hot(row == index)
    main = mm_whole(land, jnp.concatenate(plane[:2], axis=0), NN)
    rest = jnp.concatenate([plane[2][:, 0:40], plane[2][:, 40:80]], axis=0)
    rest = jnp.concatenate([rest, jnp.zeros((rest.shape[0], 24), F32)], axis=1)
    rest = mm_whole(land, rest, NN)
    part = [rest[leaf // 4 * k : leaf // 4 * (k + 1)] for k in range(4)]
    rows = jnp.concatenate(
        [
            main,
            jnp.concatenate([x[:, 0:32] for x in part], axis=1),
            jnp.concatenate([x[:, 32:64] for x in part], axis=1),
        ],
        axis=0,
    )
    rows = rows.astype(jnp.int32).astype(jnp.int16)
    for c in range(out_ref.shape[0]):
        out_ref[c] = rows


def cluster_rows(plane_ref, recv_ref, forward_ref, transposed_ref):
    devices, leaf = recv_ref.shape[0], forward_ref.shape[1]
    land = jnp.concatenate(
        [
            hot(recv_ref[:, CAP + g : CAP + g + 1] == iota((devices, leaf), 1))
            for g in range(2)
        ],
        axis=0,
    )
    first, second, rest = [
        jnp.transpose(plane_ref[r * devices : (r + 1) * devices, :]) for r in range(3)
    ]
    columns = jnp.concatenate(
        [
            jnp.concatenate([first, rest[0:40]], axis=0),
            jnp.concatenate([second, rest[40:80]], axis=0),
        ],
        axis=1,
    )
    high, low = halves(columns)
    joined = mm(high, land) * 256.0 + mm(low, land)
    forward_ref[...] = joined[:HALF] * steps_of(joined[160:161])
    transposed_ref[...] = joined[HALF:160] * steps_of(joined[161:162])


def mm_full(a, b, dims=NN):
    a0, a1, a2 = a
    b0, b1, b2 = b
    small = mm(a2, b0, dims) + mm(a1, b1, dims) + mm(a0, b2, dims)
    return (small + (mm(a1, b0, dims) + mm(a0, b1, dims))) + mm(a0, b0, dims)


def mm_hot(a, b):
    a0, a1, a2 = split3(a)
    return mm(a0, b) + mm(a1, b) + mm(a2, b)


def small_solve(p, rows):
    n = len(rows)
    p, rows, w, scaled = dict(p), list(rows), {}, []
    for i in range(0, n, 2):
        j = i + 1
        a, h, c = p[i, i], p[i, j], p[j, j]
        r = 1.0 / (a * c - h * h)
        aa, hh, cc = c * r, -(h * r), a * r
        later = range(j + 1, n)
        for m in later:
            w[i, m] = aa * p[i, m] + hh * p[j, m]
            w[j, m] = hh * p[i, m] + cc * p[j, m]
        for m in later:
            for q in range(m, n):
                p[m, q] = p[m, q] - (p[i, m] * w[i, q] + p[j, m] * w[j, q])
        for m in later:
            rows[m] = rows[m] - (w[i, m] * rows[i] + w[j, m] * rows[j])
        scaled.append(aa * rows[i] + hh * rows[j])
        scaled.append(hh * rows[i] + cc * rows[j])
    for i in range(n - 4, -1, -2):
        for q in (i, i + 1):
            for m in range(i + 2, n, 2):
                scaled[q] = scaled[q] - (w[q, m] * scaled[m] + w[q, m + 1] * scaled[m + 1])
    return scaled


def inverse(matrix):
    n, b = matrix.shape[0], 8
    a = [matrix[b * i : b * i + b] for i in range(n // b)]
    shape = a[0].shape
    sub, lane = iota(shape, 0), iota(shape, 1)
    lower, solved = [], []

    def spread(x):
        return jnp.broadcast_to(x, shape)

    for g in range(n // b):
        k = b * g
        rows = [spread(a[g][q : q + 1, :]) for q in range(b)]
        p = {
            (q, r): spread(rows[q][:, k + r : k + r + 1])
            for q in range(b)
            for r in range(q, b)
        }
        inside = jnp.logical_and(lane >= k, lane < k + b)
        rows = [
            jnp.where(inside, jnp.where(lane == k + q, 1.0, 0.0), rows[q])
            for q in range(b)
        ]
        new = small_solve(p, rows)
        left, picked = rows[0], new[0]
        for q in range(1, b):
            left = jnp.where(sub == q, rows[q], left)
            picked = jnp.where(sub == q, new[q], picked)
        lower.append(jnp.where(lane < k + b, left, 0.0))
        solved.append(jnp.where(lane < k + b, picked, 0.0))
        for i in range(g + 1, n // b):
            terms = [spread(a[i][:, k + q : k + q + 1]) * new[q] for q in range(b)]
            while len(terms) > 1:
                terms = [terms[t] + terms[t + 1] for t in range(0, len(terms), 2)]
            a[i] = jnp.where(inside, 0.0, a[i]) - terms[0]
    lower = jnp.transpose(jnp.concatenate(lower, axis=0))
    return mm_full(split3(lower), split3(jnp.concatenate(solved, axis=0)))


def leaf_kernel(
    spread_ref,
    order_ref,
    leaf_scale_ref,
    plane_ref,
    recv_ref,
    interp_ref,
    forward_ref,
    transposed_ref,
):
    cluster_rows(plane_ref, recv_ref, forward_ref, transposed_ref)
    columns = spread_ref.shape[0]
    leaf, rank = interp_ref.shape
    quarter = leaf // 4
    got = [spread_ref[c].astype(jnp.int32).astype(F32) for c in range(columns)]

    def unpacked(first):
        return jnp.concatenate(
            [
                jnp.concatenate(
                    [x[first : first + quarter, 32 * k : 32 * k + 32] for x in got],
                    axis=1,
                )
                for k in range(4)
            ],
            axis=0,
        )

    rows = jnp.concatenate([x[:leaf] for x in got] + [unpacked(leaf)], axis=1)
    steps = mm_hot(steps_of(unpacked(leaf + quarter)), leaf_scale_ref[...])
    rows = split3(rows * steps)
    pivots = [part[:rank] for part in rows]
    others = [part[rank:] for part in rows]
    eye = jnp.where(iota((rank, rank), 0) == iota((rank, rank), 1), 1.0, 0.0)
    gram = mm_full(pivots, pivots, NT) * (1.0 / (2.0 * K)) + eye
    cross = mm_full(others, pivots, NT) * (1.0 / (2.0 * K))
    chosen = order_ref[:, :rank].astype(F32)
    cross = split3(mm_split(order_ref[:, rank:], cross) - chosen)
    interp_ref[...] = chosen + mm_full(cross, split3(inverse(gram)))


def call(kernel, outs, *args, scratch=(), smem=(), hbm=(), flops=1_000_000):
    spec = [
        pl.BlockSpec(
            memory_space=pltpu.SMEM if i in smem else pltpu.HBM if i in hbm else pltpu.VMEM
        )
        for i in range(len(args))
    ]
    return pl.pallas_call(
        kernel,
        out_shape=outs,
        in_specs=spec,
        out_specs=jax.tree.map(lambda _: pl.BlockSpec(memory_space=pltpu.VMEM), outs),
        scratch_shapes=scratch,
        compiler_params=pltpu.CompilerParams(vmem_limit_bytes=48 * 2**20),
        cost_estimate=pl.CostEstimate(
            flops=flops, bytes_accessed=1_000_000, transcendentals=0
        ),
    )(*args)


def per_device(right_sample, left_sample, updates, pattern, targets, cluster_pos, pivots):
    devices = lax.axis_size("rows")
    local_rows, width = right_sample.shape
    block = updates.shape[1]
    shape = jax.ShapeDtypeStruct

    def exchange(x):
        return lax.all_to_all(x, "rows", split_axis=0, concat_axis=0, tiled=True)

    positions = cluster_pos.reshape(1, local_rows)
    message = call(
        request_kernel,
        shape((devices, 128), jnp.int32),
        pltpu.with_memory_space_constraint(targets, pltpu.HBM),
        pltpu.with_memory_space_constraint(positions, pltpu.HBM),
        hbm=(0, 1),
        scratch=[
            pltpu.VMEM((1, block), jnp.int32),
            pltpu.VMEM((1, local_rows), jnp.int32),
            pltpu.SemaphoreType.DMA((2,)),
        ],
    )
    received = exchange(message)
    prepared = call(
        prep_kernel,
        [
            shape((CAP * devices, block), BF16),
            shape((devices, block), BF16),
            shape((8, block), F32),
            shape((block, block), BF16),
            shape((devices, 128), jnp.int32),
            shape((local_rows, local_rows), BF16),
            shape((local_rows, local_rows), F32),
            shape((128, 1024), BF16),
            shape((128, 640), BF16),
        ],
        targets,
        pattern[0],
        updates[0],
        positions,
        pivots,
        smem=(1,),
    )
    received, *prepared = lax.optimization_barrier((received, *prepared))
    slots, member, rank, masked, rows, order, index, scale, leaf_scale = prepared
    reply = call(
        reply_kernel,
        shape((devices, 8, 128), BF16),
        received,
        right_sample.T,
        left_sample.T,
        scratch=[pltpu.VMEM((devices * 8, 128), F32)],
    )
    fetched = exchange(reply)
    outgoing = call(
        tile_kernel,
        shape((devices, 8, 128), jnp.int16),
        fetched,
        slots,
        member,
        rank,
        masked,
        scratch=[pltpu.VMEM((devices * 8, 128), F32)],
    )
    incoming = exchange(outgoing)
    moved = call(
        front_kernel,
        shape((devices * 4, 128), jnp.int16),
        incoming,
        received,
        rows,
        scale,
        scratch=[
            pltpu.VMEM((devices * 8, 128), F32),
            pltpu.VMEM((devices * 4, 128), F32),
        ],
    )
    arrived = exchange(moved.reshape(devices, 4, 128)).reshape(devices * 4, 128)
    columns = lax.axis_size("cols")
    packed, planes = call(
        pack_kernel,
        [
            shape((columns, local_rows * 3 // 2, 128), jnp.int16),
            shape((3 * devices, 128), F32),
        ],
        arrived,
        received,
        index,
        scratch=[pltpu.VMEM((devices * 4, 128), F32)],
    )
    spread = lax.all_to_all(packed, "cols", split_axis=0, concat_axis=0, tiled=True)
    interp, forward, transposed = call(
        leaf_kernel,
        [
            shape((local_rows, pivots.shape[1]), F32),
            shape((width, local_rows), F32),
            shape((width, local_rows), F32),
        ],
        spread,
        order,
        leaf_scale,
        planes,
        received,
    )
    return forward.T, transposed.T, interp


def solution(mesh):
    return jax.shard_map(
        per_device,
        mesh=mesh,
        in_specs=(
            P("rows", "cols"),
            P("rows", "cols"),
            P("rows", None, None),
            P("rows", None, None),
            P("rows", None),
            P("rows"),
            P("rows", None),
        ),
        out_specs=(P("rows", "cols"), P("rows", "cols"), P("rows", None)),
        check_vma=False,
    )
```

```python
import jax
import jax.numpy as jnp
from jax import lax
from jax.experimental import pallas as pl
from jax.experimental.pallas import tpu as pltpu
from jax.sharding import PartitionSpec as P

K = 320
CAP = 6
HALF = 80
CODES = 64
LOG2 = 0.6931471805599453
F32 = jnp.float32
BF16 = jnp.bfloat16
NT = (((1,), (1,)), ((), ()))
NN = (((1,), (0,)), ((), ()))


def mm(a, b, dims=NN):
    return lax.dot_general(a, b, dims, preferred_element_type=F32)


def iota(shape, dim):
    return lax.broadcasted_iota(jnp.int32, shape, dim)


def split3(x):
    hi = x.astype(BF16)
    rest = x - hi.astype(F32)
    mid = rest.astype(BF16)
    low = (rest - mid.astype(F32)).astype(BF16)
    return hi, mid, low


def hot(mask):
    return jnp.where(mask, 1.0, 0.0).astype(BF16)


def ranks(keys, devices):
    n = keys.shape[1]
    member = keys == iota((devices, n), 0)
    ahead = hot(iota((n, n), 0) < iota((n, n), 1))
    return member, mm(hot(member), ahead)


def pick(member, rank, slot, values):
    chosen = jnp.where(jnp.logical_and(member, rank == float(slot)), values, 0.0)
    return jnp.sum(chosen, axis=1, keepdims=True)


def request_kernel(targets_hbm, pos_hbm, msg_ref, targets_ref, pos_ref, arrivals):
    devices = msg_ref.shape[0]
    first = pltpu.make_async_copy(targets_hbm, targets_ref, arrivals.at[0])
    second = pltpu.make_async_copy(pos_hbm, pos_ref, arrivals.at[1])
    first.start()
    second.start()
    first.wait()
    second.wait()
    lanes = iota((devices, 128), 1)
    wanted = targets_ref[...]
    member, rank = ranks(wanted >> 8, devices)
    local = ((wanted & 255) + 1).astype(F32)
    msg = jnp.zeros((devices, 128), F32)
    for slot in range(CAP):
        msg = jnp.where(lanes == slot, pick(member, rank, slot, local) - 1.0, msg)
    pos = pos_ref[...]
    member, rank = ranks(pos >> 8, devices)
    landing = (pos & 255).astype(F32)
    for slot in range(2):
        msg = jnp.where(lanes == CAP + slot, pick(member, rank, slot, landing), msg)
    msg_ref[...] = msg.astype(jnp.int32)


def prep_kernel(
    targets_ref,
    pattern_ref,
    updates_ref,
    pos_ref,
    pivots_ref,
    slots_ref,
    member_ref,
    rank_ref,
    masked_ref,
    rows_ref,
    order_ref,
    index_ref,
    scale_ref,
    leaf_scale_ref,
):
    devices = member_ref.shape[0]
    member, rank = ranks(targets_ref[...] >> 8, devices)
    member_ref[...] = hot(member)
    rank_ref[...] = jnp.broadcast_to(
        jnp.sum(jnp.where(member, rank, 0.0), axis=0, keepdims=True), rank_ref.shape
    )
    for slot in range(CAP):
        slots_ref[slot * devices : (slot + 1) * devices, :] = hot(
            jnp.logical_and(member, rank == float(slot))
        )
    for a in range(4):
        for b in range(4):
            part = updates_ref[a * 128 : (a + 1) * 128, b * 128 : (b + 1) * 128]
            keep = pattern_ref[a, b] != 0
            masked_ref[a * 128 : (a + 1) * 128, b * 128 : (b + 1) * 128] = jnp.where(
                keep, part, jnp.zeros_like(part)
            )
    pos = pos_ref[...]
    member, rank = ranks(pos >> 8, devices)
    here = iota(pos.shape, 1).astype(F32)
    place, lane = iota((128, 128), 0), iota((128, 128), 1)
    rows = jnp.zeros(rows_ref.shape, F32)
    for slot in range(2):
        rows = jnp.where(lane == slot, pick(member, rank, slot, here), rows)
    rows_ref[...] = rows.astype(jnp.int32)
    leaf, count = order_ref.shape[0], pivots_ref.shape[1]
    pivot = iota((leaf, count), 0) == pivots_ref[...]
    other = 1.0 - jnp.sum(jnp.where(pivot, 1.0, 0.0), axis=1, keepdims=True)
    other = jnp.broadcast_to(other, (leaf, leaf - count))
    ahead = mm(hot(iota((leaf, leaf), 1) < iota((leaf, leaf), 0)), other.astype(BF16))
    order_ref[:, :count] = hot(pivot)
    order_ref[:, count:] = hot(
        jnp.logical_and(other > 0.5, ahead == iota(ahead.shape, 1).astype(F32))
    )
    place_of = jnp.where(order_ref[...] > 0.5, iota((leaf, leaf), 1).astype(F32), 0.0)
    index_ref[...] = jnp.broadcast_to(
        jnp.sum(place_of, axis=1, keepdims=True), index_ref.shape
    )
    for s in range(CAP):
        scale_ref[:, 128 * s : 128 * s + 128] = hot(
            place == CODES + s + jnp.where(lane >= HALF, 8, 0)
        )
    for s in (6, 7):
        scale_ref[:, 128 * s : 128 * s + 128] = hot(
            place == CODES + 8 + 4 * (s - 6) + (lane >> 5)
        )
    for c in range(4):
        leaf_scale_ref[:, 128 * c : 128 * c + 128] = hot(
            place == 32 * c + jnp.where(lane >= HALF, 1, 0)
        )
    leaf_scale_ref[:, 512:640] = hot(place == 32 * (lane >> 5) + 1)


def reply_kernel(recv_ref, right_ref, left_ref, out_ref, scratch):
    devices = recv_ref.shape[0]
    samples = jnp.concatenate([right_ref[...], left_ref[...]], axis=0)
    places = iota((devices, samples.shape[1]), 1)
    chosen = jnp.concatenate(
        [hot(recv_ref[:, s : s + 1] == places) for s in range(CAP)], axis=0
    )
    rows = mm(chosen, samples, NT)
    part = [rows[s * devices : (s + 1) * devices] for s in range(CAP)]
    for s in range(CAP):
        scratch[pl.ds(s, devices, stride=8), :] = part[s][:, :128]
    scratch[pl.ds(6, devices, stride=8), :] = jnp.concatenate(
        [part[s][:, 128:160] for s in range(4)], axis=1
    )
    scratch[pl.ds(7, devices, stride=8), :] = jnp.concatenate(
        [part[4][:, 128:160], part[5][:, 128:160], jnp.zeros((devices, 64), F32)], axis=1
    )
    out_ref[...] = scratch[...].reshape(out_ref.shape).astype(BF16)


def steps_of(code):
    return jnp.exp(code * (LOG2 / 256.0)) * (1.0 / 32600.0)


def code_of(peak):
    return jnp.ceil(jnp.log(jnp.maximum(peak, 1e-32)) * (256.0 / LOG2))


def coded(x):
    code = code_of(jnp.max(jnp.abs(x), axis=0, keepdims=True))
    return jnp.floor(x / steps_of(code) + 0.5), code


def halves(x):
    high = jnp.floor(x * (1.0 / 256.0) + 0.5)
    low = x - 256.0 * high
    return high.astype(BF16), low.astype(BF16)


def mm_whole(hots, x, dims=NT):
    both = mm(hots, jnp.concatenate(halves(x), axis=0 if dims == NT else 1), dims)
    n = both.shape[1] // 2
    return both[:, :n] * 256.0 + both[:, n:]


def tile_kernel(
    fetched_ref, slots_ref, member_ref, rank_ref, masked_ref, out_ref, scratch
):
    devices, columns = member_ref.shape
    scratch[...] = fetched_ref[...].astype(F32).reshape(scratch.shape)
    across = [
        jnp.transpose(scratch[pl.ds(s, devices, stride=8), :]).astype(BF16)
        for s in range(8)
    ]
    slots, member, rank = slots_ref[...], member_ref[...], rank_ref[0:1, :]
    main = mm(jnp.concatenate(across[:CAP], axis=1), slots)
    rest = mm(jnp.concatenate(across[CAP:], axis=0), member)
    tail = jnp.zeros((32, columns), F32)
    for s in range(CAP):
        tail = jnp.where(rank == float(s), rest[32 * s : 32 * s + 32], tail)
    gathered = jnp.concatenate([main, tail], axis=0).astype(BF16)
    masked = masked_ref[...]
    forward, forward_code = coded(mm(gathered[:HALF], masked, NT))
    transposed, transposed_code = coded(mm(gathered[HALF:], masked, NN))
    tail = transposed[128 - HALF :]
    row = iota((8, columns), 0).astype(F32)
    rest = jnp.concatenate(
        [jnp.where(rank == float(s), tail, 0.0) for s in range(CAP)]
        + [
            jnp.where(rank == row, forward_code, 0.0),
            jnp.where(rank == row, transposed_code, 0.0),
            jnp.zeros((48, columns), F32),
        ],
        axis=0,
    )
    main = mm_whole(slots, jnp.concatenate([forward, transposed[: 128 - HALF]], axis=0))
    rest = mm_whole(member, rest)
    for s in range(CAP):
        scratch[pl.ds(s, devices, stride=8), :] = main[s * devices : (s + 1) * devices]
    scratch[pl.ds(6, devices, stride=8), :] = rest[:, :128]
    scratch[pl.ds(7, devices, stride=8), :] = rest[:, 128:]
    out_ref[...] = (
        scratch[...].reshape(out_ref.shape).astype(jnp.int32).astype(jnp.int16)
    )


def front_kernel(incoming_ref, recv_ref, rows_ref, scale_ref, out_ref, scratch, sent):
    devices = recv_ref.shape[0]
    across = jnp.transpose(recv_ref[...].astype(F32)).astype(jnp.int32)
    move = jnp.concatenate(
        [
            jnp.concatenate(
                [
                    hot(rows_ref[:, g : g + 1] == across[s : s + 1, :])
                    for s in range(CAP)
                ],
                axis=1,
            )
            for g in range(2)
        ],
        axis=0,
    )
    scratch[...] = (
        incoming_ref[...].astype(jnp.int32).astype(F32).reshape(scratch.shape)
    )
    plane = [scratch[pl.ds(s, devices, stride=8), :] for s in range(8)]
    codes = jnp.where(iota(plane[7].shape, 1) >= CODES, plane[7], 0.0)
    scales = mm_hot(steps_of(codes), scale_ref[...])
    plane = [plane[s] * scales[:, 128 * s : 128 * s + 128] for s in range(8)]
    rest = jnp.concatenate(
        [plane[6 + s // 4][:, 32 * (s % 4) : 32 * (s % 4) + 32] for s in range(CAP)],
        axis=0,
    )
    moved = mm_split(
        move, jnp.concatenate([jnp.concatenate(plane[:CAP], axis=0), rest], axis=1)
    )
    main, rest = moved[:, :128], moved[:, 128:]
    lane = iota(main.shape, 1)
    size = jnp.abs(main)
    peaks = [
        jnp.max(jnp.where(lane < HALF, size, 0.0), axis=1, keepdims=True),
        jnp.maximum(
            jnp.max(jnp.where(lane >= HALF, size, 0.0), axis=1, keepdims=True),
            jnp.max(jnp.abs(rest), axis=1, keepdims=True),
        ),
    ]
    codes = [code_of(peak) for peak in peaks]
    steps = [1.0 / steps_of(code) for code in codes]
    main = jnp.floor(main * jnp.where(lane < HALF, steps[0], steps[1]) + 0.5)
    rest = jnp.floor(rest * steps[1] + 0.5)
    rest = jnp.concatenate(
        [
            rest[:devices],
            jnp.zeros((devices, 8), F32),
            rest[devices:],
            jnp.zeros((devices, 56), F32),
        ],
        axis=1,
    )
    lane = iota(rest.shape, 1)
    for g in range(2):
        for h in range(2):
            code = codes[h][g * devices : (g + 1) * devices]
            rest = jnp.where(lane == 40 * g + 32 + h, code, rest)
    sent[pl.ds(0, devices, stride=4), :] = main[:devices]
    sent[pl.ds(1, devices, stride=4), :] = main[devices:]
    sent[pl.ds(2, devices, stride=4), :] = rest
    sent[pl.ds(3, devices, stride=4), :] = jnp.zeros_like(rest)
    out_ref[...] = sent[...].astype(jnp.int32).astype(jnp.int16)


def mm_split(hots, x):
    x0, x1, x2 = split3(x)
    return mm(hots, x0) + mm(hots, x1) + mm(hots, x2)


def pack_kernel(arrived_ref, recv_ref, index_ref, out_ref, plane_ref, scratch):
    leaf, devices = index_ref.shape[0], recv_ref.shape[0]
    scratch[...] = arrived_ref[...].astype(jnp.int32).astype(F32)
    plane = [scratch[pl.ds(r, devices, stride=4), :] for r in range(3)]
    for r in range(3):
        plane_ref[r * devices : (r + 1) * devices, :] = plane[r]
    across = jnp.transpose(recv_ref[...].astype(F32))
    landing = jnp.concatenate([across[CAP : CAP + 1], across[CAP + 1 : CAP + 2]], axis=1)
    row = iota((leaf, landing.shape[1]), 0).astype(F32)
    index = jnp.sum(
        jnp.where(row == landing, index_ref[...], 0.0), axis=0, keepdims=True
    )
    land = hot(row == index)
    rest = jnp.concatenate([plane[2][:, 0:40], plane[2][:, 40:80]], axis=0)
    rest = jnp.concatenate([rest, jnp.zeros((rest.shape[0], 88), F32)], axis=1)
    rows = mm_whole(
        land, jnp.concatenate([jnp.concatenate(plane[:2], axis=0), rest], axis=1), NN
    )
    main, rest = rows[:, :128], rows[:, 128:]
    part = [rest[leaf // 4 * k : leaf // 4 * (k + 1)] for k in range(4)]
    rows = jnp.concatenate(
        [
            main,
            jnp.concatenate([x[:, 0:32] for x in part], axis=1),
            jnp.concatenate([x[:, 32:64] for x in part], axis=1),
        ],
        axis=0,
    )
    rows = rows.astype(jnp.int32).astype(jnp.int16)
    for c in range(out_ref.shape[0]):
        out_ref[c] = rows


def cluster_rows(plane_ref, recv_ref, forward_ref, transposed_ref):
    devices, leaf = recv_ref.shape[0], forward_ref.shape[1]
    land = jnp.concatenate(
        [
            hot(recv_ref[:, CAP + g : CAP + g + 1] == iota((devices, leaf), 1))
            for g in range(2)
        ],
        axis=0,
    )
    first, second, rest = [
        jnp.transpose(plane_ref[r * devices : (r + 1) * devices, :]) for r in range(3)
    ]
    columns = jnp.concatenate(
        [
            jnp.concatenate([first, rest[0:40]], axis=0),
            jnp.concatenate([second, rest[40:80]], axis=0),
        ],
        axis=1,
    )
    high, low = halves(columns)
    joined = mm(high, land) * 256.0 + mm(low, land)
    forward_ref[...] = joined[:HALF] * steps_of(joined[160:161])
    transposed_ref[...] = joined[HALF:160] * steps_of(joined[161:162])


def mm_full(a, b, dims=NN):
    a0, a1, a2 = a
    b0, b1, b2 = b
    small = mm(a2, b0, dims) + mm(a1, b1, dims) + mm(a0, b2, dims)
    return (small + (mm(a1, b0, dims) + mm(a0, b1, dims))) + mm(a0, b0, dims)


def mm_pair(a, b):
    a0, a1, a2 = a
    b0, b1, b2 = b
    n = b0.shape[0]
    pair = jnp.concatenate([b0, b1], axis=0)
    first, second = mm(a0, pair, NT), mm(a1, pair, NT)
    small = mm(a2, b0, NT) + mm(a0, b2, NT) + second[:, n:]
    return (small + (second[:, :n] + first[:, n:])) + first[:, :n]


def mm_hot(a, b):
    a0, a1, a2 = split3(a)
    return mm(a0, b) + mm(a1, b) + mm(a2, b)


def small_solve(p, rows):
    n = len(rows)
    p, rows, w, scaled = dict(p), list(rows), {}, []
    for i in range(0, n, 2):
        j = i + 1
        a, h, c = p[i, i], p[i, j], p[j, j]
        r = 1.0 / (a * c - h * h)
        aa, hh, cc = c * r, -(h * r), a * r
        later = range(j + 1, n)
        for m in later:
            w[i, m] = aa * p[i, m] + hh * p[j, m]
            w[j, m] = hh * p[i, m] + cc * p[j, m]
        for m in later:
            for q in range(m, n):
                p[m, q] = p[m, q] - (p[i, m] * w[i, q] + p[j, m] * w[j, q])
        for m in later:
            rows[m] = rows[m] - (w[i, m] * rows[i] + w[j, m] * rows[j])
        scaled.append(aa * rows[i] + hh * rows[j])
        scaled.append(hh * rows[i] + cc * rows[j])
    for i in range(n - 4, -1, -2):
        for q in (i, i + 1):
            for m in range(i + 2, n, 2):
                scaled[q] = scaled[q] - (w[q, m] * scaled[m] + w[q, m + 1] * scaled[m + 1])
    return scaled


def inverse(matrix):
    n, b = matrix.shape[0], 8
    a = [matrix[b * i : b * i + b] for i in range(n // b)]
    shape = a[0].shape
    sub, lane = iota(shape, 0), iota(shape, 1)
    lower, solved = [], []
    zero = jnp.zeros(shape, F32)

    def spread(x):
        return jnp.broadcast_to(x, shape)

    for g in range(n // b):
        k = b * g
        rows = [spread(a[g][q : q + 1, :]) for q in range(b)]
        p = {
            (q, r): spread(rows[q][:, k + r : k + r + 1])
            for q in range(b)
            for r in range(q, b)
        }
        inside = jnp.logical_and(lane >= k, lane < k + b)
        rows = [
            jnp.where(inside, jnp.where(lane == k + q, 1.0, 0.0), rows[q])
            for q in range(b)
        ]
        new = small_solve(p, rows)
        left, picked = rows[0], new[0]
        for q in range(1, b):
            left = jnp.where(sub == q, rows[q], left)
            picked = jnp.where(sub == q, new[q], picked)
        lower.append(jnp.where(lane < k + b, left, 0.0))
        solved.append(jnp.where(lane < k + b, picked, 0.0))
        if g + 1 < n // b:
            terms = [spread(a[g + 1][:, k + q : k + q + 1]) * new[q] for q in range(b)]
            while len(terms) > 1:
                terms = [terms[t] + terms[t + 1] for t in range(0, len(terms), 2)]
            a[g + 1] = jnp.where(inside, 0.0, a[g + 1]) - terms[0]
        if g + 2 < n // b:
            x0, x1, x2 = split3(jnp.concatenate(a[g + 2 :], axis=0))
            y0, y1, y2 = split3(
                jnp.concatenate([picked if i == g else zero for i in range(n // b)], axis=0)
            )
            change = mm(
                jnp.concatenate([x0, x0, x0, x1, x1, x2], axis=1),
                jnp.concatenate([y0, y1, y2, y0, y1, y0], axis=0),
            )
            for i in range(g + 2, n // b):
                first = b * (i - g - 2)
                a[i] = jnp.where(inside, 0.0, a[i]) - change[first : first + b]
    lower = jnp.transpose(jnp.concatenate(lower, axis=0))
    return mm_full(split3(lower), split3(jnp.concatenate(solved, axis=0)))


def leaf_kernel(
    spread_ref,
    order_ref,
    leaf_scale_ref,
    plane_ref,
    recv_ref,
    interp_ref,
    forward_ref,
    transposed_ref,
):
    cluster_rows(plane_ref, recv_ref, forward_ref, transposed_ref)
    columns = spread_ref.shape[0]
    leaf, rank = interp_ref.shape
    quarter = leaf // 4
    got = [spread_ref[c].astype(jnp.int32).astype(F32) for c in range(columns)]

    def unpacked(first):
        return jnp.concatenate(
            [
                jnp.concatenate(
                    [x[first : first + quarter, 32 * k : 32 * k + 32] for x in got],
                    axis=1,
                )
                for k in range(4)
            ],
            axis=0,
        )

    rows = jnp.concatenate([x[:leaf] for x in got] + [unpacked(leaf)], axis=1)
    steps = mm_hot(steps_of(unpacked(leaf + quarter)), leaf_scale_ref[...])
    rows = split3(rows * steps)
    pivots = [part[:rank] for part in rows]
    others = [part[rank:] for part in rows]
    eye = jnp.where(iota((rank, rank), 0) == iota((rank, rank), 1), 1.0, 0.0)
    gram = mm_pair(pivots, pivots) * (1.0 / (2.0 * K)) + eye
    cross = mm_pair(others, pivots) * (1.0 / (2.0 * K))
    chosen = order_ref[:, :rank].astype(F32)
    cross = split3(mm_split(order_ref[:, rank:], cross) - chosen)
    interp_ref[...] = chosen + mm_full(cross, split3(inverse(gram)))


def call(kernel, outs, *args, scratch=(), smem=(), hbm=(), flops=1_000_000):
    spec = [
        pl.BlockSpec(
            memory_space=pltpu.SMEM if i in smem else pltpu.HBM if i in hbm else pltpu.VMEM
        )
        for i in range(len(args))
    ]
    return pl.pallas_call(
        kernel,
        out_shape=outs,
        in_specs=spec,
        out_specs=jax.tree.map(lambda _: pl.BlockSpec(memory_space=pltpu.VMEM), outs),
        scratch_shapes=scratch,
        compiler_params=pltpu.CompilerParams(vmem_limit_bytes=48 * 2**20),
        cost_estimate=pl.CostEstimate(
            flops=flops, bytes_accessed=1_000_000, transcendentals=0
        ),
    )(*args)


def per_device(right_sample, left_sample, updates, pattern, targets, cluster_pos, pivots):
    devices = lax.axis_size("rows")
    local_rows, width = right_sample.shape
    block = updates.shape[1]
    shape = jax.ShapeDtypeStruct

    def exchange(x):
        return lax.all_to_all(x, "rows", split_axis=0, concat_axis=0, tiled=True)

    positions = cluster_pos.reshape(1, local_rows)
    message = call(
        request_kernel,
        shape((devices, 128), jnp.int32),
        pltpu.with_memory_space_constraint(targets, pltpu.HBM),
        pltpu.with_memory_space_constraint(positions, pltpu.HBM),
        hbm=(0, 1),
        scratch=[
            pltpu.VMEM((1, block), jnp.int32),
            pltpu.VMEM((1, local_rows), jnp.int32),
            pltpu.SemaphoreType.DMA((2,)),
        ],
    )
    received = exchange(message)
    prepared = call(
        prep_kernel,
        [
            shape((CAP * devices, block), BF16),
            shape((devices, block), BF16),
            shape((8, block), F32),
            shape((block, block), BF16),
            shape((devices, 128), jnp.int32),
            shape((local_rows, local_rows), BF16),
            shape((local_rows, local_rows), F32),
            shape((128, 1024), BF16),
            shape((128, 640), BF16),
        ],
        targets,
        pattern[0],
        updates[0],
        positions,
        pivots,
        smem=(1,),
    )
    received, *prepared = lax.optimization_barrier((received, *prepared))
    slots, member, rank, masked, rows, order, index, scale, leaf_scale = prepared
    reply = call(
        reply_kernel,
        shape((devices, 8, 128), BF16),
        received,
        right_sample.T,
        left_sample.T,
        scratch=[pltpu.VMEM((devices * 8, 128), F32)],
    )
    fetched = exchange(reply)
    outgoing = call(
        tile_kernel,
        shape((devices, 8, 128), jnp.int16),
        fetched,
        slots,
        member,
        rank,
        masked,
        scratch=[pltpu.VMEM((devices * 8, 128), F32)],
    )
    incoming = exchange(outgoing)
    moved = call(
        front_kernel,
        shape((devices * 4, 128), jnp.int16),
        incoming,
        received,
        rows,
        scale,
        scratch=[
            pltpu.VMEM((devices * 8, 128), F32),
            pltpu.VMEM((devices * 4, 128), F32),
        ],
    )
    arrived = exchange(moved.reshape(devices, 4, 128)).reshape(devices * 4, 128)
    columns = lax.axis_size("cols")
    packed, planes = call(
        pack_kernel,
        [
            shape((columns, local_rows * 3 // 2, 128), jnp.int16),
            shape((3 * devices, 128), F32),
        ],
        arrived,
        received,
        index,
        scratch=[pltpu.VMEM((devices * 4, 128), F32)],
    )
    spread = lax.all_to_all(packed, "cols", split_axis=0, concat_axis=0, tiled=True)
    interp, forward, transposed = call(
        leaf_kernel,
        [
            shape((local_rows, pivots.shape[1]), F32),
            shape((width, local_rows), F32),
            shape((width, local_rows), F32),
        ],
        spread,
        order,
        leaf_scale,
        planes,
        received,
    )
    return forward.T, transposed.T, interp


def solution(mesh):
    return jax.shard_map(
        per_device,
        mesh=mesh,
        in_specs=(
            P("rows", "cols"),
            P("rows", "cols"),
            P("rows", None, None),
            P("rows", None, None),
            P("rows", None),
            P("rows"),
            P("rows", None),
        ),
        out_specs=(P("rows", "cols"), P("rows", "cols"), P("rows", None)),
        check_vma=False,
    )
```

```python
import jax
import jax.numpy as jnp
from jax import lax
from jax.experimental import pallas as pl
from jax.experimental.pallas import tpu as pltpu
from jax.sharding import PartitionSpec as P

K = 320
CAP = 6
HALF = 80
CODES = 64
LOG2 = 0.6931471805599453
F32 = jnp.float32
BF16 = jnp.bfloat16
NT = (((1,), (1,)), ((), ()))
NN = (((1,), (0,)), ((), ()))


def mm(a, b, dims=NN):
    return lax.dot_general(a, b, dims, preferred_element_type=F32)


def iota(shape, dim):
    return lax.broadcasted_iota(jnp.int32, shape, dim)


def split3(x):
    hi = x.astype(BF16)
    rest = x - hi.astype(F32)
    mid = rest.astype(BF16)
    low = (rest - mid.astype(F32)).astype(BF16)
    return hi, mid, low


def hot(mask):
    return jnp.where(mask, 1.0, 0.0).astype(BF16)


def ranks(keys, devices):
    n = keys.shape[1]
    member = keys == iota((devices, n), 0)
    ahead = hot(iota((n, n), 0) < iota((n, n), 1))
    return member, mm(hot(member), ahead)


def pick(member, rank, slot, values):
    chosen = jnp.where(jnp.logical_and(member, rank == float(slot)), values, 0.0)
    return jnp.sum(chosen, axis=1, keepdims=True)


def request_kernel(targets_hbm, pos_hbm, msg_ref, targets_ref, pos_ref, arrivals):
    devices = msg_ref.shape[0]
    first = pltpu.make_async_copy(targets_hbm, targets_ref, arrivals.at[0])
    second = pltpu.make_async_copy(pos_hbm, pos_ref, arrivals.at[1])
    first.start()
    second.start()
    first.wait()
    second.wait()
    lanes = iota((devices, 128), 1)
    wanted = targets_ref[...]
    member, rank = ranks(wanted >> 8, devices)
    local = ((wanted & 255) + 1).astype(F32)
    msg = jnp.zeros((devices, 128), F32)
    for slot in range(CAP):
        msg = jnp.where(lanes == slot, pick(member, rank, slot, local) - 1.0, msg)
    pos = pos_ref[...]
    member, rank = ranks(pos >> 8, devices)
    landing = (pos & 255).astype(F32)
    for slot in range(2):
        msg = jnp.where(lanes == CAP + slot, pick(member, rank, slot, landing), msg)
    msg_ref[...] = msg.astype(jnp.int32)


def prep_kernel(
    targets_ref,
    pattern_ref,
    updates_ref,
    pos_ref,
    pivots_ref,
    slots_ref,
    member_ref,
    rank_ref,
    masked_ref,
    rows_ref,
    order_ref,
    index_ref,
    scale_ref,
    leaf_scale_ref,
):
    devices = member_ref.shape[0]
    member, rank = ranks(targets_ref[...] >> 8, devices)
    member_ref[...] = hot(member)
    rank_ref[...] = jnp.broadcast_to(
        jnp.sum(jnp.where(member, rank, 0.0), axis=0, keepdims=True), rank_ref.shape
    )
    for slot in range(CAP):
        slots_ref[slot * devices : (slot + 1) * devices, :] = hot(
            jnp.logical_and(member, rank == float(slot))
        )
    for a in range(4):
        for b in range(4):
            part = updates_ref[a * 128 : (a + 1) * 128, b * 128 : (b + 1) * 128]
            keep = pattern_ref[a, b] != 0
            masked_ref[a * 128 : (a + 1) * 128, b * 128 : (b + 1) * 128] = jnp.where(
                keep, part, jnp.zeros_like(part)
            )
    pos = pos_ref[...]
    member, rank = ranks(pos >> 8, devices)
    here = iota(pos.shape, 1).astype(F32)
    place, lane = iota((128, 128), 0), iota((128, 128), 1)
    rows = jnp.zeros(rows_ref.shape, F32)
    for slot in range(2):
        rows = jnp.where(lane == slot, pick(member, rank, slot, here), rows)
    rows_ref[...] = rows.astype(jnp.int32)
    leaf, count = order_ref.shape[0], pivots_ref.shape[1]
    pivot = iota((leaf, count), 0) == pivots_ref[...]
    other = 1.0 - jnp.sum(jnp.where(pivot, 1.0, 0.0), axis=1, keepdims=True)
    other = jnp.broadcast_to(other, (leaf, leaf - count))
    ahead = mm(hot(iota((leaf, leaf), 1) < iota((leaf, leaf), 0)), other.astype(BF16))
    order_ref[:, :count] = hot(pivot)
    order_ref[:, count:] = hot(
        jnp.logical_and(other > 0.5, ahead == iota(ahead.shape, 1).astype(F32))
    )
    place_of = jnp.where(order_ref[...] > 0.5, iota((leaf, leaf), 1).astype(F32), 0.0)
    index_ref[...] = jnp.broadcast_to(
        jnp.sum(place_of, axis=1, keepdims=True), index_ref.shape
    )
    for s in range(CAP):
        scale_ref[:, 128 * s : 128 * s + 128] = hot(
            place == CODES + s + jnp.where(lane >= HALF, 8, 0)
        )
    for s in (6, 7):
        scale_ref[:, 128 * s : 128 * s + 128] = hot(
            place == CODES + 8 + 4 * (s - 6) + (lane >> 5)
        )
    for c in range(4):
        leaf_scale_ref[:, 128 * c : 128 * c + 128] = hot(
            place == 8 * c + jnp.where(lane >= HALF, 1, 0)
        )
    leaf_scale_ref[:, 512:640] = hot(place == 8 * (lane >> 5) + 1)


def reply_kernel(recv_ref, right_ref, left_ref, out_ref, scratch):
    devices = recv_ref.shape[0]
    samples = jnp.concatenate([right_ref[...], left_ref[...]], axis=0)
    places = iota((devices, samples.shape[1]), 1)
    chosen = jnp.concatenate(
        [hot(recv_ref[:, s : s + 1] == places) for s in range(CAP)], axis=0
    )
    rows = mm(chosen, samples, NT)
    part = [rows[s * devices : (s + 1) * devices] for s in range(CAP)]
    for s in range(CAP):
        scratch[pl.ds(s, devices, stride=8), :] = part[s][:, :128]
    scratch[pl.ds(6, devices, stride=8), :] = jnp.concatenate(
        [part[s][:, 128:160] for s in range(4)], axis=1
    )
    scratch[pl.ds(7, devices, stride=8), :] = jnp.concatenate(
        [part[4][:, 128:160], part[5][:, 128:160], jnp.zeros((devices, 64), F32)], axis=1
    )
    out_ref[...] = scratch[...].reshape(out_ref.shape).astype(BF16)


def steps_of(code):
    return jnp.exp(code * (LOG2 / 256.0)) * (1.0 / 32600.0)


def code_of(peak):
    return jnp.ceil(jnp.log(jnp.maximum(peak, 1e-32)) * (256.0 / LOG2))


def coded(x):
    code = code_of(jnp.max(jnp.abs(x), axis=0, keepdims=True))
    return jnp.floor(x / steps_of(code) + 0.5), code


def halves(x):
    high = jnp.floor(x * (1.0 / 256.0) + 0.5)
    low = x - 256.0 * high
    return high.astype(BF16), low.astype(BF16)


def mm_whole(hots, x, dims=NT):
    both = mm(hots, jnp.concatenate(halves(x), axis=0 if dims == NT else 1), dims)
    n = both.shape[1] // 2
    return both[:, :n] * 256.0 + both[:, n:]


def tile_kernel(
    fetched_ref, slots_ref, member_ref, rank_ref, masked_ref, out_ref, scratch
):
    devices, columns = member_ref.shape
    scratch[...] = fetched_ref[...].astype(F32).reshape(scratch.shape)
    across = [
        jnp.transpose(scratch[pl.ds(s, devices, stride=8), :]).astype(BF16)
        for s in range(8)
    ]
    slots, member, rank = slots_ref[...], member_ref[...], rank_ref[0:1, :]
    main = mm(jnp.concatenate(across[:CAP], axis=1), slots)
    rest = mm(jnp.concatenate(across[CAP:], axis=0), member)
    tail = jnp.zeros((32, columns), F32)
    for s in range(CAP):
        tail = jnp.where(rank == float(s), rest[32 * s : 32 * s + 32], tail)
    gathered = jnp.concatenate([main, tail], axis=0).astype(BF16)
    masked = masked_ref[...]
    forward, forward_code = coded(mm(gathered[:HALF], masked, NT))
    transposed, transposed_code = coded(mm(gathered[HALF:], masked, NN))
    tail = transposed[128 - HALF :]
    row = iota((8, columns), 0).astype(F32)
    rest = jnp.concatenate(
        [jnp.where(rank == float(s), tail, 0.0) for s in range(CAP)]
        + [
            jnp.where(rank == row, forward_code, 0.0),
            jnp.where(rank == row, transposed_code, 0.0),
            jnp.zeros((48, columns), F32),
        ],
        axis=0,
    )
    main = mm_whole(slots, jnp.concatenate([forward, transposed[: 128 - HALF]], axis=0))
    rest = mm_whole(member, rest)
    for s in range(CAP):
        scratch[pl.ds(s, devices, stride=8), :] = main[s * devices : (s + 1) * devices]
    scratch[pl.ds(6, devices, stride=8), :] = rest[:, :128]
    scratch[pl.ds(7, devices, stride=8), :] = rest[:, 128:]
    out_ref[...] = (
        scratch[...].reshape(out_ref.shape).astype(jnp.int32).astype(jnp.int16)
    )


def front_kernel(incoming_ref, recv_ref, rows_ref, scale_ref, out_ref, scratch, sent):
    devices = recv_ref.shape[0]
    across = jnp.transpose(recv_ref[...].astype(F32)).astype(jnp.int32)
    move = jnp.concatenate(
        [
            jnp.concatenate(
                [
                    hot(rows_ref[:, g : g + 1] == across[s : s + 1, :])
                    for s in range(CAP)
                ],
                axis=1,
            )
            for g in range(2)
        ],
        axis=0,
    )
    scratch[...] = (
        incoming_ref[...].astype(jnp.int32).astype(F32).reshape(scratch.shape)
    )
    plane = [scratch[pl.ds(s, devices, stride=8), :] for s in range(8)]
    codes = jnp.where(iota(plane[7].shape, 1) >= CODES, plane[7], 0.0)
    scales = mm_hot(steps_of(codes), scale_ref[...])
    plane = [plane[s] * scales[:, 128 * s : 128 * s + 128] for s in range(8)]
    rest = jnp.concatenate(
        [plane[6 + s // 4][:, 32 * (s % 4) : 32 * (s % 4) + 32] for s in range(CAP)],
        axis=0,
    )
    moved = mm_split(
        move, jnp.concatenate([jnp.concatenate(plane[:CAP], axis=0), rest], axis=1)
    )
    main, rest = moved[:, :128], moved[:, 128:]
    lane = iota(main.shape, 1)
    size = jnp.abs(main)
    peaks = [
        jnp.max(jnp.where(lane < HALF, size, 0.0), axis=1, keepdims=True),
        jnp.maximum(
            jnp.max(jnp.where(lane >= HALF, size, 0.0), axis=1, keepdims=True),
            jnp.max(jnp.abs(rest), axis=1, keepdims=True),
        ),
    ]
    codes = [code_of(peak) for peak in peaks]
    steps = [1.0 / steps_of(code) for code in codes]
    main = jnp.floor(main * jnp.where(lane < HALF, steps[0], steps[1]) + 0.5)
    rest = jnp.floor(rest * steps[1] + 0.5)
    rest = jnp.concatenate(
        [
            rest[:devices],
            jnp.zeros((devices, 8), F32),
            rest[devices:],
            jnp.zeros((devices, 56), F32),
        ],
        axis=1,
    )
    lane = iota(rest.shape, 1)
    for g in range(2):
        for h in range(2):
            code = codes[h][g * devices : (g + 1) * devices]
            rest = jnp.where(lane == 40 * g + 32 + h, code, rest)
    sent[pl.ds(0, devices, stride=4), :] = main[:devices]
    sent[pl.ds(1, devices, stride=4), :] = main[devices:]
    sent[pl.ds(2, devices, stride=4), :] = rest
    sent[pl.ds(3, devices, stride=4), :] = jnp.zeros_like(rest)
    out_ref[...] = sent[...].astype(jnp.int32).astype(jnp.int16)


def mm_split(hots, x):
    x0, x1, x2 = split3(x)
    return mm(hots, x0) + mm(hots, x1) + mm(hots, x2)


def pack_kernel(arrived_ref, recv_ref, index_ref, out_ref, plane_ref, scratch):
    leaf, devices = index_ref.shape[0], recv_ref.shape[0]
    scratch[...] = arrived_ref[...].astype(jnp.int32).astype(F32)
    plane = [scratch[pl.ds(r, devices, stride=4), :] for r in range(3)]
    for r in range(3):
        plane_ref[r * devices : (r + 1) * devices, :] = plane[r]
    across = jnp.transpose(recv_ref[...].astype(F32))
    landing = jnp.concatenate([across[CAP : CAP + 1], across[CAP + 1 : CAP + 2]], axis=1)
    row = iota((leaf, landing.shape[1]), 0).astype(F32)
    index = jnp.sum(
        jnp.where(row == landing, index_ref[...], 0.0), axis=0, keepdims=True
    )
    land = hot(row == index)
    rest = jnp.concatenate([plane[2][:, 0:40], plane[2][:, 40:80]], axis=0)
    rest = jnp.concatenate([rest, jnp.zeros((rest.shape[0], 88), F32)], axis=1)
    rows = mm_whole(
        land, jnp.concatenate([jnp.concatenate(plane[:2], axis=0), rest], axis=1), NN
    )
    main, rest = rows[:, :128], rows[:, 128:]
    part = [rest[leaf // 4 * k : leaf // 4 * (k + 1)] for k in range(4)]
    rows = jnp.concatenate(
        [
            main,
            jnp.concatenate([x[:, 0:32] for x in part], axis=1),
            jnp.concatenate(
                [rest[16 * k : 16 * k + 16, 32:40] for k in range(leaf // 16)], axis=1
            ),
        ],
        axis=0,
    )
    rows = rows.astype(jnp.int32).astype(jnp.int16)
    for c in range(out_ref.shape[0]):
        out_ref[c] = rows


def cluster_rows(plane_ref, recv_ref, forward_ref, transposed_ref):
    devices, leaf = recv_ref.shape[0], forward_ref.shape[1]
    land = jnp.concatenate(
        [
            hot(recv_ref[:, CAP + g : CAP + g + 1] == iota((devices, leaf), 1))
            for g in range(2)
        ],
        axis=0,
    )
    first, second, rest = [
        jnp.transpose(plane_ref[r * devices : (r + 1) * devices, :]) for r in range(3)
    ]
    columns = jnp.concatenate(
        [
            jnp.concatenate([first, rest[0:40]], axis=0),
            jnp.concatenate([second, rest[40:80]], axis=0),
        ],
        axis=1,
    )
    high, low = halves(columns)
    joined = mm(high, land) * 256.0 + mm(low, land)
    forward_ref[...] = joined[:HALF] * steps_of(joined[160:161])
    transposed_ref[...] = joined[HALF:160] * steps_of(joined[161:162])


def mm_full(a, b, dims=NN):
    a0, a1, a2 = a
    b0, b1, b2 = b
    return mm(
        jnp.concatenate([a2, a1, a0, a1, a0, a0], axis=1),
        jnp.concatenate([b0, b1, b2, b0, b1, b0], axis=1 if dims == NT else 0),
        dims,
    )


def mm_pair(a, b):
    a0, a1, a2 = a
    b0, b1, b2 = b
    n = b0.shape[0]
    pair = jnp.concatenate([b0, b1], axis=0)
    first, second = mm(a0, pair, NT), mm(a1, pair, NT)
    small = mm(a2, b0, NT) + mm(a0, b2, NT) + second[:, n:]
    return (small + (second[:, :n] + first[:, n:])) + first[:, :n]


def mm_hot(a, b):
    a0, a1, a2 = split3(a)
    return mm(a0, b) + mm(a1, b) + mm(a2, b)


def small_solve(p, rows):
    n = len(rows)
    p, rows, w, scaled = dict(p), list(rows), {}, []
    for i in range(0, n, 2):
        j = i + 1
        a, h, c = p[i, i], p[i, j], p[j, j]
        r = 1.0 / (a * c - h * h)
        aa, hh, cc = c * r, -(h * r), a * r
        later = range(j + 1, n)
        for m in later:
            w[i, m] = aa * p[i, m] + hh * p[j, m]
            w[j, m] = hh * p[i, m] + cc * p[j, m]
        for m in later:
            for q in range(m, n):
                p[m, q] = p[m, q] - (p[i, m] * w[i, q] + p[j, m] * w[j, q])
        for m in later:
            rows[m] = rows[m] - (w[i, m] * rows[i] + w[j, m] * rows[j])
        scaled.append(aa * rows[i] + hh * rows[j])
        scaled.append(hh * rows[i] + cc * rows[j])
    for i in range(n - 4, -1, -2):
        for q in (i, i + 1):
            for m in range(i + 2, n, 2):
                scaled[q] = scaled[q] - (w[q, m] * scaled[m] + w[q, m + 1] * scaled[m + 1])
    return scaled


def inverse(matrix):
    n, b = matrix.shape[0], 8
    a = [matrix[b * i : b * i + b] for i in range(n // b)]
    shape = a[0].shape
    sub, lane = iota(shape, 0), iota(shape, 1)
    lower, solved = [], []
    zero = jnp.zeros(shape, F32)

    def spread(x):
        return jnp.broadcast_to(x, shape)

    for g in range(n // b):
        k = b * g
        rows = [spread(a[g][q : q + 1, :]) for q in range(b)]
        p = {
            (q, r): spread(rows[q][:, k + r : k + r + 1])
            for q in range(b)
            for r in range(q, b)
        }
        inside = jnp.logical_and(lane >= k, lane < k + b)
        rows = [
            jnp.where(inside, jnp.where(lane == k + q, 1.0, 0.0), rows[q])
            for q in range(b)
        ]
        new = small_solve(p, rows)
        left, picked = rows[0], new[0]
        for q in range(1, b):
            left = jnp.where(sub == q, rows[q], left)
            picked = jnp.where(sub == q, new[q], picked)
        lower.append(jnp.where(lane < k + b, left, 0.0))
        solved.append(jnp.where(lane < k + b, picked, 0.0))
        if g + 1 < n // b:
            terms = [spread(a[g + 1][:, k + q : k + q + 1]) * new[q] for q in range(b)]
            while len(terms) > 1:
                terms = [terms[t] + terms[t + 1] for t in range(0, len(terms), 2)]
            a[g + 1] = jnp.where(inside, 0.0, a[g + 1]) - terms[0]
        if g + 2 < n // b:
            x0, x1, x2 = split3(jnp.concatenate(a[g + 2 :], axis=0))
            y0, y1, y2 = split3(
                jnp.concatenate([picked if i == g else zero for i in range(n // b)], axis=0)
            )
            change = mm(
                jnp.concatenate([x0, x0, x0, x1, x1, x2], axis=1),
                jnp.concatenate([y0, y1, y2, y0, y1, y0], axis=0),
            )
            for i in range(g + 2, n // b):
                first = b * (i - g - 2)
                a[i] = jnp.where(inside, 0.0, a[i]) - change[first : first + b]
    lower = jnp.transpose(jnp.concatenate(lower, axis=0))
    return mm_full(split3(lower), split3(jnp.concatenate(solved, axis=0)))


def leaf_kernel(
    spread_ref,
    order_ref,
    leaf_scale_ref,
    plane_ref,
    recv_ref,
    interp_ref,
    forward_ref,
    transposed_ref,
):
    columns = spread_ref.shape[0]
    leaf, rank = interp_ref.shape
    quarter = leaf // 4
    got = [spread_ref[c].astype(jnp.int32).astype(F32) for c in range(columns)]

    def unpacked(first, count, width):
        return jnp.concatenate(
            [
                jnp.concatenate(
                    [x[first : first + count, width * k : width * k + width] for x in got],
                    axis=1,
                )
                for k in range(leaf // count)
            ],
            axis=0,
        )

    rest = unpacked(leaf, quarter, 32)
    rows = jnp.concatenate([x[:leaf] for x in got] + [rest], axis=1)
    codes = unpacked(leaf + quarter, 16, 8)
    steps = mm_hot(steps_of(codes), leaf_scale_ref[: codes.shape[1], :])
    rows = split3(rows * steps)
    pivots = [part[:rank] for part in rows]
    others = [part[rank:] for part in rows]
    eye = jnp.where(iota((rank, rank), 0) == iota((rank, rank), 1), 1.0, 0.0)
    gram = mm_pair(pivots, pivots) * (1.0 / (2.0 * K)) + eye
    cross = mm_pair(others, pivots) * (1.0 / (2.0 * K))
    cluster_rows(plane_ref, recv_ref, forward_ref, transposed_ref)
    chosen = order_ref[:, :rank].astype(F32)
    cross = split3(mm_split(order_ref[:, rank:], cross) - chosen)
    interp_ref[...] = chosen + mm_full(cross, split3(inverse(gram)))


def call(kernel, outs, *args, scratch=(), smem=(), hbm=(), flops=1_000_000):
    spec = [
        pl.BlockSpec(
            memory_space=pltpu.SMEM if i in smem else pltpu.HBM if i in hbm else pltpu.VMEM
        )
        for i in range(len(args))
    ]
    return pl.pallas_call(
        kernel,
        out_shape=outs,
        in_specs=spec,
        out_specs=jax.tree.map(lambda _: pl.BlockSpec(memory_space=pltpu.VMEM), outs),
        scratch_shapes=scratch,
        compiler_params=pltpu.CompilerParams(vmem_limit_bytes=48 * 2**20),
        cost_estimate=pl.CostEstimate(
            flops=flops, bytes_accessed=1_000_000, transcendentals=0
        ),
    )(*args)


def per_device(right_sample, left_sample, updates, pattern, targets, cluster_pos, pivots):
    devices = lax.axis_size("rows")
    local_rows, width = right_sample.shape
    block = updates.shape[1]
    shape = jax.ShapeDtypeStruct

    def exchange(x):
        return lax.all_to_all(x, "rows", split_axis=0, concat_axis=0, tiled=True)

    positions = cluster_pos.reshape(1, local_rows)
    message = call(
        request_kernel,
        shape((devices, 128), jnp.int32),
        pltpu.with_memory_space_constraint(targets, pltpu.HBM),
        pltpu.with_memory_space_constraint(positions, pltpu.HBM),
        hbm=(0, 1),
        scratch=[
            pltpu.VMEM((1, block), jnp.int32),
            pltpu.VMEM((1, local_rows), jnp.int32),
            pltpu.SemaphoreType.DMA((2,)),
        ],
    )
    received = exchange(message)
    prepared = call(
        prep_kernel,
        [
            shape((CAP * devices, block), BF16),
            shape((devices, block), BF16),
            shape((8, block), F32),
            shape((block, block), BF16),
            shape((devices, 128), jnp.int32),
            shape((local_rows, local_rows), BF16),
            shape((local_rows, local_rows), F32),
            shape((128, 1024), BF16),
            shape((128, 640), BF16),
        ],
        targets,
        pattern[0],
        updates[0],
        positions,
        pivots,
        smem=(1,),
    )
    received, *prepared = lax.optimization_barrier((received, *prepared))
    slots, member, rank, masked, rows, order, index, scale, leaf_scale = prepared
    reply = call(
        reply_kernel,
        shape((devices, 8, 128), BF16),
        received,
        right_sample.T,
        left_sample.T,
        scratch=[pltpu.VMEM((devices * 8, 128), F32)],
    )
    fetched = exchange(reply)
    outgoing = call(
        tile_kernel,
        shape((devices, 8, 128), jnp.int16),
        fetched,
        slots,
        member,
        rank,
        masked,
        scratch=[pltpu.VMEM((devices * 8, 128), F32)],
    )
    incoming = exchange(outgoing)
    moved = call(
        front_kernel,
        shape((devices * 4, 128), jnp.int16),
        incoming,
        received,
        rows,
        scale,
        scratch=[
            pltpu.VMEM((devices * 8, 128), F32),
            pltpu.VMEM((devices * 4, 128), F32),
        ],
    )
    arrived = exchange(moved.reshape(devices, 4, 128)).reshape(devices * 4, 128)
    columns = lax.axis_size("cols")
    packed, planes = call(
        pack_kernel,
        [
            shape((columns, local_rows * 5 // 4 + 16, 128), jnp.int16),
            shape((3 * devices, 128), F32),
        ],
        arrived,
        received,
        index,
        scratch=[pltpu.VMEM((devices * 4, 128), F32)],
    )
    spread = lax.all_to_all(packed, "cols", split_axis=0, concat_axis=0, tiled=True)
    interp, forward, transposed = call(
        leaf_kernel,
        [
            shape((local_rows, pivots.shape[1]), F32),
            shape((width, local_rows), F32),
            shape((width, local_rows), F32),
        ],
        spread,
        order,
        leaf_scale,
        planes,
        received,
    )
    return forward.T, transposed.T, interp


def solution(mesh):
    return jax.shard_map(
        per_device,
        mesh=mesh,
        in_specs=(
            P("rows", "cols"),
            P("rows", "cols"),
            P("rows", None, None),
            P("rows", None, None),
            P("rows", None),
            P("rows"),
            P("rows", None),
        ),
        out_specs=(P("rows", "cols"), P("rows", "cols"), P("rows", None)),
        check_vma=False,
    )
```

```python
import jax
import jax.numpy as jnp
from jax import lax
from jax.experimental import pallas as pl
from jax.experimental.pallas import tpu as pltpu
from jax.sharding import PartitionSpec as P

K = 320
CAP = 6
HALF = 80
CODES = 64
AHEAD = 2
LOG2 = 0.6931471805599453
F32 = jnp.float32
BF16 = jnp.bfloat16
NT = (((1,), (1,)), ((), ()))
NN = (((1,), (0,)), ((), ()))


def mm(a, b, dims=NN):
    return lax.dot_general(a, b, dims, preferred_element_type=F32)


def iota(shape, dim):
    return lax.broadcasted_iota(jnp.int32, shape, dim)


def split3(x):
    hi = x.astype(BF16)
    rest = x - hi.astype(F32)
    mid = rest.astype(BF16)
    low = (rest - mid.astype(F32)).astype(BF16)
    return hi, mid, low


def hot(mask):
    return jnp.where(mask, 1.0, 0.0).astype(BF16)


def ranks(keys, devices):
    n = keys.shape[1]
    member = keys == iota((devices, n), 0)
    ahead = hot(iota((n, n), 0) < iota((n, n), 1))
    return member, mm(hot(member), ahead)


def pick(member, rank, slot, values):
    chosen = jnp.where(jnp.logical_and(member, rank == float(slot)), values, 0.0)
    return jnp.sum(chosen, axis=1, keepdims=True)


def request_kernel(targets_hbm, pos_hbm, msg_ref, targets_ref, pos_ref, arrivals):
    devices = msg_ref.shape[0]
    first = pltpu.make_async_copy(targets_hbm, targets_ref, arrivals.at[0])
    second = pltpu.make_async_copy(pos_hbm, pos_ref, arrivals.at[1])
    first.start()
    second.start()
    first.wait()
    second.wait()
    lanes = iota((devices, 128), 1)
    wanted = targets_ref[...]
    member, rank = ranks(wanted >> 8, devices)
    local = ((wanted & 255) + 1).astype(F32)
    msg = jnp.zeros((devices, 128), F32)
    for slot in range(CAP):
        msg = jnp.where(lanes == slot, pick(member, rank, slot, local) - 1.0, msg)
    pos = pos_ref[...]
    member, rank = ranks(pos >> 8, devices)
    landing = (pos & 255).astype(F32)
    for slot in range(2):
        msg = jnp.where(lanes == CAP + slot, pick(member, rank, slot, landing), msg)
    msg_ref[...] = msg.astype(jnp.int32)


def prep_kernel(
    targets_ref,
    pattern_ref,
    updates_ref,
    pos_ref,
    pivots_ref,
    slots_ref,
    member_ref,
    rank_ref,
    masked_ref,
    rows_ref,
    order_ref,
    index_ref,
    scale_ref,
    leaf_scale_ref,
):
    devices = member_ref.shape[0]
    member, rank = ranks(targets_ref[...] >> 8, devices)
    member_ref[...] = hot(member)
    rank_ref[...] = jnp.broadcast_to(
        jnp.sum(jnp.where(member, rank, 0.0), axis=0, keepdims=True), rank_ref.shape
    )
    for slot in range(CAP):
        slots_ref[slot * devices : (slot + 1) * devices, :] = hot(
            jnp.logical_and(member, rank == float(slot))
        )
    for a in range(4):
        for b in range(4):
            part = updates_ref[a * 128 : (a + 1) * 128, b * 128 : (b + 1) * 128]
            keep = pattern_ref[a, b] != 0
            masked_ref[a * 128 : (a + 1) * 128, b * 128 : (b + 1) * 128] = jnp.where(
                keep, part, jnp.zeros_like(part)
            )
    pos = pos_ref[...]
    member, rank = ranks(pos >> 8, devices)
    here = iota(pos.shape, 1).astype(F32)
    place, lane = iota((128, 128), 0), iota((128, 128), 1)
    rows = jnp.zeros(rows_ref.shape, F32)
    for slot in range(2):
        rows = jnp.where(lane == slot, pick(member, rank, slot, here), rows)
    rows_ref[...] = rows.astype(jnp.int32)
    leaf, count = order_ref.shape[0], pivots_ref.shape[1]
    pivot = iota((leaf, count), 0) == pivots_ref[...]
    other = 1.0 - jnp.sum(jnp.where(pivot, 1.0, 0.0), axis=1, keepdims=True)
    other = jnp.broadcast_to(other, (leaf, leaf - count))
    ahead = mm(hot(iota((leaf, leaf), 1) < iota((leaf, leaf), 0)), other.astype(BF16))
    order_ref[:, :count] = hot(pivot)
    order_ref[:, count:] = hot(
        jnp.logical_and(other > 0.5, ahead == iota(ahead.shape, 1).astype(F32))
    )
    place_of = jnp.where(order_ref[...] > 0.5, iota((leaf, leaf), 1).astype(F32), 0.0)
    index_ref[...] = jnp.broadcast_to(
        jnp.sum(place_of, axis=1, keepdims=True), index_ref.shape
    )
    for s in range(CAP):
        scale_ref[:, 128 * s : 128 * s + 128] = hot(
            place == CODES + s + jnp.where(lane >= HALF, 8, 0)
        )
    for s in (6, 7):
        scale_ref[:, 128 * s : 128 * s + 128] = hot(
            place == CODES + 8 + 4 * (s - 6) + (lane >> 5)
        )
    for c in range(4):
        leaf_scale_ref[:, 128 * c : 128 * c + 128] = hot(
            place == 8 * c + jnp.where(lane >= HALF, 1, 0)
        )
    leaf_scale_ref[:, 512:640] = hot(place == 8 * (lane >> 5) + 1)


def reply_kernel(recv_ref, right_ref, left_ref, out_ref, scratch):
    devices = recv_ref.shape[0]
    samples = jnp.concatenate([right_ref[...], left_ref[...]], axis=0)
    places = iota((devices, samples.shape[1]), 1)
    chosen = jnp.concatenate(
        [hot(recv_ref[:, s : s + 1] == places) for s in range(CAP)], axis=0
    )
    rows = mm(chosen, samples, NT)
    part = [rows[s * devices : (s + 1) * devices] for s in range(CAP)]
    for s in range(CAP):
        scratch[pl.ds(s, devices, stride=8), :] = part[s][:, :128]
    scratch[pl.ds(6, devices, stride=8), :] = jnp.concatenate(
        [part[s][:, 128:160] for s in range(4)], axis=1
    )
    scratch[pl.ds(7, devices, stride=8), :] = jnp.concatenate(
        [part[4][:, 128:160], part[5][:, 128:160], jnp.zeros((devices, 64), F32)], axis=1
    )
    out_ref[...] = scratch[...].reshape(out_ref.shape).astype(BF16)


def steps_of(code):
    return jnp.exp(code * (LOG2 / 256.0)) * (1.0 / 32600.0)


def code_of(peak):
    return jnp.ceil(jnp.log(jnp.maximum(peak, 1e-32)) * (256.0 / LOG2))


def coded(x):
    code = code_of(jnp.max(jnp.abs(x), axis=0, keepdims=True))
    return jnp.floor(x / steps_of(code) + 0.5), code


def halves(x):
    high = jnp.floor(x * (1.0 / 256.0) + 0.5)
    low = x - 256.0 * high
    return high.astype(BF16), low.astype(BF16)


def mm_whole(hots, x, dims=NT):
    both = mm(hots, jnp.concatenate(halves(x), axis=0 if dims == NT else 1), dims)
    n = both.shape[1] // 2
    return both[:, :n] * 256.0 + both[:, n:]


def tile_kernel(
    fetched_ref, slots_ref, member_ref, rank_ref, masked_ref, out_ref, scratch
):
    devices, columns = member_ref.shape
    scratch[...] = fetched_ref[...].astype(F32).reshape(scratch.shape)
    across = [
        jnp.transpose(scratch[pl.ds(s, devices, stride=8), :]).astype(BF16)
        for s in range(8)
    ]
    slots, member, rank = slots_ref[...], member_ref[...], rank_ref[0:1, :]
    main = mm(jnp.concatenate(across[:CAP], axis=1), slots)
    rest = mm(jnp.concatenate(across[CAP:], axis=0), member)
    tail = jnp.zeros((32, columns), F32)
    for s in range(CAP):
        tail = jnp.where(rank == float(s), rest[32 * s : 32 * s + 32], tail)
    gathered = jnp.concatenate([main, tail], axis=0).astype(BF16)
    masked = masked_ref[...]
    forward, forward_code = coded(mm(gathered[:HALF], masked, NT))
    transposed, transposed_code = coded(mm(gathered[HALF:], masked, NN))
    tail = transposed[128 - HALF :]
    row = iota((8, columns), 0).astype(F32)
    rest = jnp.concatenate(
        [jnp.where(rank == float(s), tail, 0.0) for s in range(CAP)]
        + [
            jnp.where(rank == row, forward_code, 0.0),
            jnp.where(rank == row, transposed_code, 0.0),
            jnp.zeros((48, columns), F32),
        ],
        axis=0,
    )
    main = mm_whole(slots, jnp.concatenate([forward, transposed[: 128 - HALF]], axis=0))
    rest = mm_whole(member, rest)
    for s in range(CAP):
        scratch[pl.ds(s, devices, stride=8), :] = main[s * devices : (s + 1) * devices]
    scratch[pl.ds(6, devices, stride=8), :] = rest[:, :128]
    scratch[pl.ds(7, devices, stride=8), :] = rest[:, 128:]
    out_ref[...] = (
        scratch[...].reshape(out_ref.shape).astype(jnp.int32).astype(jnp.int16)
    )


def front_kernel(incoming_ref, recv_ref, rows_ref, scale_ref, out_ref, scratch, sent):
    devices = recv_ref.shape[0]
    across = jnp.transpose(recv_ref[...].astype(F32)).astype(jnp.int32)
    move = jnp.concatenate(
        [
            jnp.concatenate(
                [
                    hot(rows_ref[:, g : g + 1] == across[s : s + 1, :])
                    for s in range(CAP)
                ],
                axis=1,
            )
            for g in range(2)
        ],
        axis=0,
    )
    scratch[...] = (
        incoming_ref[...].astype(jnp.int32).astype(F32).reshape(scratch.shape)
    )
    plane = [scratch[pl.ds(s, devices, stride=8), :] for s in range(8)]
    codes = jnp.where(iota(plane[7].shape, 1) >= CODES, plane[7], 0.0)
    scales = mm_hot(steps_of(codes), scale_ref[...])
    plane = [plane[s] * scales[:, 128 * s : 128 * s + 128] for s in range(8)]
    rest = jnp.concatenate(
        [plane[6 + s // 4][:, 32 * (s % 4) : 32 * (s % 4) + 32] for s in range(CAP)],
        axis=0,
    )
    moved = mm_split(
        move, jnp.concatenate([jnp.concatenate(plane[:CAP], axis=0), rest], axis=1)
    )
    main, rest = moved[:, :128], moved[:, 128:]
    lane = iota(main.shape, 1)
    size = jnp.abs(main)
    peaks = [
        jnp.max(jnp.where(lane < HALF, size, 0.0), axis=1, keepdims=True),
        jnp.maximum(
            jnp.max(jnp.where(lane >= HALF, size, 0.0), axis=1, keepdims=True),
            jnp.max(jnp.abs(rest), axis=1, keepdims=True),
        ),
    ]
    codes = [code_of(peak) for peak in peaks]
    steps = [1.0 / steps_of(code) for code in codes]
    main = jnp.floor(main * jnp.where(lane < HALF, steps[0], steps[1]) + 0.5)
    rest = jnp.floor(rest * steps[1] + 0.5)
    rest = jnp.concatenate(
        [
            rest[:devices],
            jnp.zeros((devices, 8), F32),
            rest[devices:],
            jnp.zeros((devices, 56), F32),
        ],
        axis=1,
    )
    lane = iota(rest.shape, 1)
    for g in range(2):
        for h in range(2):
            code = codes[h][g * devices : (g + 1) * devices]
            rest = jnp.where(lane == 40 * g + 32 + h, code, rest)
    sent[pl.ds(0, devices, stride=4), :] = main[:devices]
    sent[pl.ds(1, devices, stride=4), :] = main[devices:]
    sent[pl.ds(2, devices, stride=4), :] = rest
    sent[pl.ds(3, devices, stride=4), :] = jnp.zeros_like(rest)
    out_ref[...] = sent[...].astype(jnp.int32).astype(jnp.int16)


def mm_split(hots, x):
    x0, x1, x2 = split3(x)
    return mm(hots, x0) + mm(hots, x1) + mm(hots, x2)


def pack_kernel(arrived_ref, recv_ref, index_ref, out_ref, plane_ref, scratch):
    leaf, devices = index_ref.shape[0], recv_ref.shape[0]
    scratch[...] = arrived_ref[...].astype(jnp.int32).astype(F32)
    plane = [scratch[pl.ds(r, devices, stride=4), :] for r in range(3)]
    for r in range(3):
        plane_ref[r * devices : (r + 1) * devices, :] = plane[r]
    across = jnp.transpose(recv_ref[...].astype(F32))
    landing = jnp.concatenate([across[CAP : CAP + 1], across[CAP + 1 : CAP + 2]], axis=1)
    row = iota((leaf, landing.shape[1]), 0).astype(F32)
    index = jnp.sum(
        jnp.where(row == landing, index_ref[...], 0.0), axis=0, keepdims=True
    )
    land = hot(row == index)
    rest = jnp.concatenate([plane[2][:, 0:40], plane[2][:, 40:80]], axis=0)
    rest = jnp.concatenate([rest, jnp.zeros((rest.shape[0], 88), F32)], axis=1)
    rows = mm_whole(
        land, jnp.concatenate([jnp.concatenate(plane[:2], axis=0), rest], axis=1), NN
    )
    main, rest = rows[:, :128], rows[:, 128:]
    part = [rest[leaf // 4 * k : leaf // 4 * (k + 1)] for k in range(4)]
    rows = jnp.concatenate(
        [
            main,
            jnp.concatenate([x[:, 0:32] for x in part], axis=1),
            jnp.concatenate(
                [rest[16 * k : 16 * k + 16, 32:40] for k in range(leaf // 16)], axis=1
            ),
        ],
        axis=0,
    )
    rows = rows.astype(jnp.int32).astype(jnp.int16)
    for c in range(out_ref.shape[0]):
        out_ref[c] = rows


def cluster_rows(plane_ref, recv_ref, forward_ref, transposed_ref):
    devices, leaf = recv_ref.shape[0], forward_ref.shape[1]
    land = jnp.concatenate(
        [
            hot(recv_ref[:, CAP + g : CAP + g + 1] == iota((devices, leaf), 1))
            for g in range(2)
        ],
        axis=0,
    )
    first, second, rest = [
        jnp.transpose(plane_ref[r * devices : (r + 1) * devices, :]) for r in range(3)
    ]
    columns = jnp.concatenate(
        [
            jnp.concatenate([first, rest[0:40]], axis=0),
            jnp.concatenate([second, rest[40:80]], axis=0),
        ],
        axis=1,
    )
    high, low = halves(columns)
    joined = mm(high, land) * 256.0 + mm(low, land)
    forward_ref[...] = joined[:HALF] * steps_of(joined[160:161])
    transposed_ref[...] = joined[HALF:160] * steps_of(joined[161:162])


def mm_full(a, b, dims=NN):
    a0, a1, a2 = a
    b0, b1, b2 = b
    return mm(
        jnp.concatenate([a2, a1, a0, a1, a0, a0], axis=1),
        jnp.concatenate([b0, b1, b2, b0, b1, b0], axis=1 if dims == NT else 0),
        dims,
    )


def mm_pair(a, b):
    a0, a1, a2 = a
    b0, b1, b2 = b
    n = b0.shape[0]
    pair = jnp.concatenate([b0, b1], axis=0)
    first, second = mm(a0, pair, NT), mm(a1, pair, NT)
    small = mm(a2, b0, NT) + mm(a0, b2, NT) + second[:, n:]
    return (small + (second[:, :n] + first[:, n:])) + first[:, :n]


def mm_hot(a, b):
    a0, a1, a2 = split3(a)
    return mm(a0, b) + mm(a1, b) + mm(a2, b)


def small_solve(p, rows):
    n = len(rows)
    p, rows, w, scaled = dict(p), list(rows), {}, []
    for i in range(0, n, 2):
        j = i + 1
        a, h, c = p[i, i], p[i, j], p[j, j]
        r = 1.0 / (a * c - h * h)
        aa, hh, cc = c * r, -(h * r), a * r
        later = range(j + 1, n)
        for m in later:
            w[i, m] = aa * p[i, m] + hh * p[j, m]
            w[j, m] = hh * p[i, m] + cc * p[j, m]
        for m in later:
            for q in range(m, n):
                p[m, q] = p[m, q] - (p[i, m] * w[i, q] + p[j, m] * w[j, q])
        for m in later:
            rows[m] = rows[m] - (w[i, m] * rows[i] + w[j, m] * rows[j])
        scaled.append(aa * rows[i] + hh * rows[j])
        scaled.append(hh * rows[i] + cc * rows[j])
    for i in range(n - 4, -1, -2):
        for q in (i, i + 1):
            for m in range(i + 2, n, 2):
                scaled[q] = scaled[q] - (w[q, m] * scaled[m] + w[q, m + 1] * scaled[m + 1])
    return scaled


def inverse(matrix):
    n, b = matrix.shape[0], 8
    a = [matrix[b * i : b * i + b] for i in range(n // b)]
    shape = a[0].shape
    sub, lane = iota(shape, 0), iota(shape, 1)
    lower, solved = [], []
    zero = jnp.zeros(shape, F32)

    def spread(x):
        return jnp.broadcast_to(x, shape)

    for g in range(n // b):
        k = b * g
        rows = [spread(a[g][q : q + 1, :]) for q in range(b)]
        p = {
            (q, r): spread(rows[q][:, k + r : k + r + 1])
            for q in range(b)
            for r in range(q, b)
        }
        inside = jnp.logical_and(lane >= k, lane < k + b)
        rows = [
            jnp.where(inside, jnp.where(lane == k + q, 1.0, 0.0), rows[q])
            for q in range(b)
        ]
        new = small_solve(p, rows)
        left, picked = rows[0], new[0]
        for q in range(1, b):
            left = jnp.where(sub == q, rows[q], left)
            picked = jnp.where(sub == q, new[q], picked)
        lower.append(jnp.where(lane < k + b, left, 0.0))
        solved.append(jnp.where(lane < k + b, picked, 0.0))
        behind = min(g + 1 + AHEAD, n // b)
        for i in range(g + 1, behind):
            terms = [spread(a[i][:, k + q : k + q + 1]) * new[q] for q in range(b)]
            while len(terms) > 1:
                terms = [terms[t] + terms[t + 1] for t in range(0, len(terms), 2)]
            a[i] = jnp.where(inside, 0.0, a[i]) - terms[0]
        if behind < n // b:
            x0, x1, x2 = split3(jnp.concatenate(a[behind:], axis=0))
            y0, y1, y2 = split3(
                jnp.concatenate([picked if i == g else zero for i in range(n // b)], axis=0)
            )
            change = mm(
                jnp.concatenate([x0, x0, x0, x1, x1, x2], axis=1),
                jnp.concatenate([y0, y1, y2, y0, y1, y0], axis=0),
            )
            for i in range(behind, n // b):
                first = b * (i - behind)
                a[i] = jnp.where(inside, 0.0, a[i]) - change[first : first + b]
    lower = jnp.transpose(jnp.concatenate(lower, axis=0))
    return mm_full(split3(lower), split3(jnp.concatenate(solved, axis=0)))


def leaf_kernel(
    spread_ref,
    order_ref,
    leaf_scale_ref,
    plane_ref,
    recv_ref,
    interp_ref,
    forward_ref,
    transposed_ref,
):
    columns = spread_ref.shape[0]
    leaf, rank = interp_ref.shape
    quarter = leaf // 4
    got = [spread_ref[c].astype(jnp.int32).astype(F32) for c in range(columns)]

    def unpacked(first, count, width):
        return jnp.concatenate(
            [
                jnp.concatenate(
                    [x[first : first + count, width * k : width * k + width] for x in got],
                    axis=1,
                )
                for k in range(leaf // count)
            ],
            axis=0,
        )

    rest = unpacked(leaf, quarter, 32)
    rows = jnp.concatenate([x[:leaf] for x in got] + [rest], axis=1)
    codes = unpacked(leaf + quarter, 16, 8)
    steps = mm_hot(steps_of(codes), leaf_scale_ref[: codes.shape[1], :])
    rows = split3(rows * steps)
    pivots = [part[:rank] for part in rows]
    others = [part[rank:] for part in rows]
    eye = jnp.where(iota((rank, rank), 0) == iota((rank, rank), 1), 1.0, 0.0)
    gram = mm_pair(pivots, pivots) * (1.0 / (2.0 * K)) + eye
    cross = mm_pair(others, pivots) * (1.0 / (2.0 * K))
    cluster_rows(plane_ref, recv_ref, forward_ref, transposed_ref)
    chosen = order_ref[:, :rank].astype(F32)
    cross = split3(mm_split(order_ref[:, rank:], cross) - chosen)
    interp_ref[...] = chosen + mm_full(cross, split3(inverse(gram)))


def call(kernel, outs, *args, scratch=(), smem=(), hbm=(), flops=1_000_000):
    spec = [
        pl.BlockSpec(
            memory_space=pltpu.SMEM if i in smem else pltpu.HBM if i in hbm else pltpu.VMEM
        )
        for i in range(len(args))
    ]
    return pl.pallas_call(
        kernel,
        out_shape=outs,
        in_specs=spec,
        out_specs=jax.tree.map(lambda _: pl.BlockSpec(memory_space=pltpu.VMEM), outs),
        scratch_shapes=scratch,
        compiler_params=pltpu.CompilerParams(vmem_limit_bytes=48 * 2**20),
        cost_estimate=pl.CostEstimate(
            flops=flops, bytes_accessed=1_000_000, transcendentals=0
        ),
    )(*args)


def per_device(right_sample, left_sample, updates, pattern, targets, cluster_pos, pivots):
    devices = lax.axis_size("rows")
    local_rows, width = right_sample.shape
    block = updates.shape[1]
    shape = jax.ShapeDtypeStruct

    def exchange(x):
        return lax.all_to_all(x, "rows", split_axis=0, concat_axis=0, tiled=True)

    positions = cluster_pos.reshape(1, local_rows)
    message = call(
        request_kernel,
        shape((devices, 128), jnp.int32),
        pltpu.with_memory_space_constraint(targets, pltpu.HBM),
        pltpu.with_memory_space_constraint(positions, pltpu.HBM),
        hbm=(0, 1),
        scratch=[
            pltpu.VMEM((1, block), jnp.int32),
            pltpu.VMEM((1, local_rows), jnp.int32),
            pltpu.SemaphoreType.DMA((2,)),
        ],
    )
    received = exchange(message)
    prepared = call(
        prep_kernel,
        [
            shape((CAP * devices, block), BF16),
            shape((devices, block), BF16),
            shape((8, block), F32),
            shape((block, block), BF16),
            shape((devices, 128), jnp.int32),
            shape((local_rows, local_rows), BF16),
            shape((local_rows, local_rows), F32),
            shape((128, 1024), BF16),
            shape((128, 640), BF16),
        ],
        targets,
        pattern[0],
        updates[0],
        positions,
        pivots,
        smem=(1,),
    )
    received, *prepared = lax.optimization_barrier((received, *prepared))
    slots, member, rank, masked, rows, order, index, scale, leaf_scale = prepared
    reply = call(
        reply_kernel,
        shape((devices, 8, 128), BF16),
        received,
        right_sample.T,
        left_sample.T,
        scratch=[pltpu.VMEM((devices * 8, 128), F32)],
    )
    fetched = exchange(reply)
    outgoing = call(
        tile_kernel,
        shape((devices, 8, 128), jnp.int16),
        fetched,
        slots,
        member,
        rank,
        masked,
        scratch=[pltpu.VMEM((devices * 8, 128), F32)],
    )
    incoming = exchange(outgoing)
    moved = call(
        front_kernel,
        shape((devices * 4, 128), jnp.int16),
        incoming,
        received,
        rows,
        scale,
        scratch=[
            pltpu.VMEM((devices * 8, 128), F32),
            pltpu.VMEM((devices * 4, 128), F32),
        ],
    )
    arrived = exchange(moved.reshape(devices, 4, 128)).reshape(devices * 4, 128)
    columns = lax.axis_size("cols")
    packed, planes = call(
        pack_kernel,
        [
            shape((columns, local_rows * 5 // 4 + 16, 128), jnp.int16),
            shape((3 * devices, 128), F32),
        ],
        arrived,
        received,
        index,
        scratch=[pltpu.VMEM((devices * 4, 128), F32)],
    )
    spread = lax.all_to_all(packed, "cols", split_axis=0, concat_axis=0, tiled=True)
    interp, forward, transposed = call(
        leaf_kernel,
        [
            shape((local_rows, pivots.shape[1]), F32),
            shape((width, local_rows), F32),
            shape((width, local_rows), F32),
        ],
        spread,
        order,
        leaf_scale,
        planes,
        received,
    )
    return forward.T, transposed.T, interp


def solution(mesh):
    return jax.shard_map(
        per_device,
        mesh=mesh,
        in_specs=(
            P("rows", "cols"),
            P("rows", "cols"),
            P("rows", None, None),
            P("rows", None, None),
            P("rows", None),
            P("rows"),
            P("rows", None),
        ),
        out_specs=(P("rows", "cols"), P("rows", "cols"), P("rows", None)),
        check_vma=False,
    )
```
